256 devices in a mesh: dp: 16 (over z_hi, y, core), seq: 16 (over x, z_lo).
Axes of the slice: x: 4, y: 4, z: 8 (z_hi: 2, z_lo: 4; z = z_hi * 4 + z_lo), core: 2. Of those that a mesh axis runs over, the one named last changes fastest.
Arguments:
- hidden: bfloat16 [16, 2048, 7168], P('dp', 'seq'), may hold values from -6 to 6
- queries: bfloat16 [16, 2048, 2, 4096], P('dp', 'seq'), may hold values from -7 to 7
- keys: bfloat16 [16, 2048, 1024], P('dp', 'seq'), may hold values from -7 to 7
- cotangent: bfloat16 [16, 2048, 2, 4096], P('dp', 'seq'), may hold values from -6 to 6
- segments: int32 [16, 2048], P('dp'), may hold values from 0 to 7, never falling along the last dimension, each value on 1 to 512 neighbouring positions
- weight: bfloat16 [1024, 7168], P(None, 'seq'), may hold values from -6 to 6
- master: float32 [1024, 7168], P('dp', 'seq'), may hold values from -6 to 6
- first_moment: float32 [1024, 7168], P('dp', 'seq'), may hold values from -6 to 6
- second_moment: float32 [1024, 7168], P('dp', 'seq'), may hold values from 0.5 to 4
Outputs:
- attention: bfloat16 [16, 2, 2048, 4096], P('dp', None, None, 'seq')
- new_master: float32 [1024, 7168], P('dp', 'seq')
- new_first: float32 [1024, 7168], P('dp', 'seq')
- new_second: float32 [1024, 7168], P('dp', 'seq')
- new_weight: bfloat16 [1024, 7168], P(None, 'seq')
The draws below stay inside these ranges and needn't reach their ends.
All inputs are finite; a program needn't handle non-finite values.
Results may differ from the reference program's by a relative error of at most 0.024.
Values may be sent and summed in bfloat16 or wider, within the bound.
No kernel may reach another device: no remote copies, remote signals or barrier semaphores. Data moves between devices by JAX's collectives and lax.ppermute only.
A program may use at most 128 MiB of HBM per device.

```python
import math
import jax
import jax.numpy as jnp
import numpy as np
from jax import lax

D = 7168
QH = 32
KVH = 8
HD = 128
LENGTH = 2048
SEQS = 16
VW = 1024
N_SEQ = 16


def draw_queries(key, part):
    key = jax.random.fold_in(key, 5)
    shape = (SEQS, LENGTH, 2, QH, HD)
    base = jax.random.truncated_normal(key, -6.0, 6.0, shape, jnp.float32)
    return base.reshape(SEQS, LENGTH, 2, QH * HD).astype(jnp.bfloat16)


def draw_keys(key, part):
    key = jax.random.fold_in(key, 6)
    shape = (SEQS, LENGTH, KVH, HD)
    base = jax.random.truncated_normal(key, -6.0, 6.0, shape, jnp.float32)
    return base.reshape(SEQS, LENGTH, KVH * HD).astype(jnp.bfloat16)


def block_levels(rng, dims, cuts, low, high):
    loudness = 1.0
    for axis_at, blocks in cuts:
        draws = jax.random.uniform(jax.random.fold_in(jax.random.fold_in(rng, 6), axis_at), (blocks,), jnp.float32, low / len(cuts), high / len(cuts))
        loudness = loudness * jnp.repeat(jnp.exp(draws), dims[axis_at] // blocks).reshape((-1,) + (1,) * (len(dims) - 1 - axis_at))
    return loudness


def length_profile(amount, total, reach, lean):
    loads = [(1 << 20) // math.isqrt(grade ** lean) + 1 for grade in range(2, amount + 1)]
    spare, holding = total - reach - (amount - 1), [1] * (amount - 1)
    while spare > 0:
        free = [i for i in range(amount - 1) if holding[i] < reach]
        pool, left = sum([loads[i] for i in free]), spare
        for i in free:
            more = min(reach - holding[i], max(1, left * loads[i] // pool), spare)
            holding[i] = holding[i] + more
            spare = spare - more
    return np.array([reach] + holding)


def ragged_sizes(key, count, total, bound, skew):
    if count == 2:
        one = jax.random.randint(key, (), max(1, total - bound), min(bound, total - 1) + 1)
        return jnp.stack([one, total - one])
    lengths = jnp.asarray(length_profile(count, total, bound, skew), jnp.int32)
    couples = (count - 1) // 2
    source_of, taker = lengths[1:1 + 2 * couples:2], lengths[2:2 + 2 * couples:2]
    margin = jnp.minimum(source_of - 1, bound - taker)
    moved = jax.random.randint(jax.random.fold_in(key, 1), (couples,), 0, 1 << 20) % (margin + 1)
    lengths = lengths.at[1:1 + 2 * couples:2].set(source_of - moved).at[2:2 + 2 * couples:2].set(taker + moved)
    return lengths[jax.random.permutation(jax.random.fold_in(key, 2), count)]


def noise(stream_key, extent, deviation, limit, cuts=(), dtype=jnp.bfloat16):
    entries = deviation * jax.random.normal(stream_key, extent, jnp.float32)
    if cuts:
        entries = entries * block_levels(stream_key, extent, cuts, -0.22, 0.18)
    return jnp.clip(entries, -limit, limit).astype(dtype)


def setup_inputs(seed: int = 0) -> dict:
    streams_of = jax.random.split(jax.random.key(seed), 10)
    return {
        "hidden": noise(streams_of[0], (SEQS, LENGTH, D), 1.0, 6.0, ((0, 16), (1, 16))),
        "queries": draw_queries(jax.random.fold_in(streams_of[9], 71), 0),
        "keys": draw_keys(jax.random.fold_in(streams_of[9], 71), 0),
        "cotangent": noise(streams_of[3], (SEQS, LENGTH, 2, QH * HD), 1.0, 6.0, ((0, 16), (1, 16))),
        "segments": jax.vmap(lambda own: jnp.searchsorted(jnp.cumsum(ragged_sizes(own, 8, LENGTH, LENGTH // 4, 0)), jnp.arange(LENGTH), side="right"))(jax.random.split(streams_of[4], SEQS)).reshape((SEQS, LENGTH)).astype(jnp.int32),
        "weight": noise(streams_of[5], (VW, D), 1.0, 6.0, ((1, 16),)),
        "master": noise(streams_of[6], (VW, D), 1.0, 6.0, ((0, 16), (1, 16)), jnp.float32),
        "first_moment": noise(streams_of[7], (VW, D), 1.0, 6.0, ((0, 16), (1, 16)), jnp.float32),
        "second_moment": jnp.clip(jnp.exp(math.log(4.0) - 2.0794415 * jax.random.uniform(streams_of[8], (VW, D), jnp.float32) ** block_levels(streams_of[8], (VW, D), ((0, 16), (1, 16)), -0.2, 0.2)), 0.5, 4.0),
    }


beta_one = 0.9
beta_two = 0.95
rate = 0.05
stability_offset = 1e-08
first_fix = 1.0 - 0.9 ** 20
second_fix = 1.0 - 0.95 ** 20

def adam_update(gradient, master, first_moment, second_moment):
    new_first = beta_one * first_moment + (1.0 - beta_one) * gradient
    new_second = beta_two * second_moment + (1.0 - beta_two) * gradient * gradient
    step_size = new_first / first_fix / (jnp.sqrt(new_second / second_fix) + stability_offset)
    new_master = master - rate * step_size
    return (new_master, new_first, new_second)

def reference(hidden, queries, keys, cotangent, segments, weight, master, first_moment, second_moment):
    scale = D ** (-0.5)
    head_scale = HD ** (-0.5)
    repeat = N_SEQ // KVH
    per_key_value = QH // KVH
    local_heads = QH // N_SEQ
    feat_block = D // N_SEQ
    weight_blocks = weight.astype(jnp.float32).reshape(VW, N_SEQ, feat_block)
    kv_of_head = (jnp.arange(2 * QH) % QH // per_key_value).astype(jnp.int32)
    positions = jnp.arange(LENGTH)

    def one_sequence(total, item):
        rows, query, key_rows, gradient_list, seg = item
        parts = jnp.einsum('snf,cnf->nsc', rows.astype(jnp.float32).reshape(LENGTH, N_SEQ, feat_block), weight_blocks) * scale
        parts = lax.optimization_barrier(parts.astype(jnp.bfloat16))
        value_tensors = lax.optimization_barrier(jnp.sum(parts.astype(jnp.float32), axis=0)).astype(jnp.bfloat16).reshape(LENGTH, KVH, HD)
        key_heads = key_rows.reshape(LENGTH, KVH, HD)
        allowed = (seg[:, None] == seg[None, :]) & (positions[:, None] >= positions[None, :])
        query_heads = query.reshape(LENGTH, 2 * QH, HD).transpose(1, 0, 2)
        grad_heads = gradient_list.reshape(LENGTH, 2 * QH, HD).transpose(1, 0, 2)

        def one_head(head_item):
            query_one, grad_one, kv_index = head_item
            key_one = lax.dynamic_index_in_dim(key_heads, kv_index, 1, keepdims=False)
            value_one = lax.dynamic_index_in_dim(value_tensors, kv_index, 1, keepdims=False)
            scores = jnp.dot(query_one, key_one.T, preferred_element_type=jnp.float32) * head_scale
            scores = jnp.where(allowed, scores, -jnp.inf)
            row_max = lax.optimization_barrier(jnp.max(scores, axis=1, keepdims=True))
            exp_scores = jnp.exp(scores - row_max)
            probabilities = (exp_scores / lax.optimization_barrier(jnp.sum(exp_scores, axis=1, keepdims=True))).astype(jnp.bfloat16)
            output = jnp.dot(probabilities, value_one, preferred_element_type=jnp.float32).astype(jnp.bfloat16)
            contrib = jnp.dot(probabilities.T, grad_one, preferred_element_type=jnp.float32)
            return (output, contrib)
        outputs, contribs = lax.map(one_head, (query_heads, grad_heads, kv_of_head))
        group_sums = lax.optimization_barrier(jnp.sum(contribs.reshape(2, N_SEQ, local_heads, LENGTH, HD), axis=(0, 2)))
        group_parts = lax.optimization_barrier(group_sums.astype(jnp.bfloat16))
        value_grad = lax.optimization_barrier(jnp.sum(group_parts.astype(jnp.float32).reshape(KVH, repeat, LENGTH, HD), axis=1)).astype(jnp.bfloat16)
        grad_rows = value_grad.transpose(1, 0, 2).reshape(LENGTH, VW)
        gradient = jnp.dot(grad_rows.T, rows, preferred_element_type=jnp.float32) * scale
        attention = outputs.reshape(2, QH, LENGTH, HD).transpose(0, 2, 1, 3).reshape(2, LENGTH, QH * HD)
        return (total + gradient, attention)
    gradient, attention = lax.scan(one_sequence, jnp.zeros((VW, D), jnp.float32), (hidden, queries, keys, cotangent, segments))
    new_master, new_first, new_second = adam_update(gradient, master, first_moment, second_moment)
    return (attention, new_master, new_first, new_second, new_master.astype(jnp.bfloat16))
```

```python
import jax
import jax.numpy as jnp
from jax import lax
from jax.experimental import pallas as pl
from jax.experimental.pallas import tpu as pltpu
from jax.sharding import Mesh, PartitionSpec as P

D = 7168
KVH = 8
HD = 128
BLOCK = 128
BACK = 5
FEATS = D // 4
LOG2E = 1.4426950408889634
MASKED = -1e30
VMEM_LIMIT = 48 * 1024 * 1024

beta_one = 0.9
beta_two = 0.95
rate = 0.05
stability_offset = 1e-08
first_fix = 1.0 - 0.9**20
second_fix = 1.0 - 0.95**20

bf16 = jnp.bfloat16
f32 = jnp.float32
DP = ("zh", "y", "core")
SEQ = ("x", "z")


def adam_update(gradient, master, first_moment, second_moment):
    new_first = beta_one * first_moment + (1.0 - beta_one) * gradient
    new_second = beta_two * second_moment + (1.0 - beta_two) * gradient * gradient
    step_size = new_first / first_fix / (jnp.sqrt(new_second / second_fix) + stability_offset)
    new_master = master - rate * step_size
    return (new_master, new_first, new_second)


def params(**more):
    return pltpu.CompilerParams(vmem_limit_bytes=VMEM_LIMIT, **more)


def cost(flops, nbytes, exps=0):
    return pl.CostEstimate(flops=flops, bytes_accessed=nbytes, transcendentals=exps)


def pack_columns(rows):
    tokens, width = rows.shape
    part = width // 4

    def body(in_ref, out_ref):
        out_ref[0] = in_ref[...]

    return pl.pallas_call(
        body,
        grid=(4,),
        in_specs=[pl.BlockSpec((tokens, part), lambda i: (0, i))],
        out_specs=pl.BlockSpec((1, tokens, part), lambda i: (i, 0, 0)),
        out_shape=jax.ShapeDtypeStruct((4, tokens, part), rows.dtype),
        compiler_params=params(),
        cost_estimate=cost(0, 4 * tokens * width),
        name="pack_columns",
    )(rows)


def pack_layers(rows):
    tokens, layers, width = rows.shape
    part = width // 4

    def body(in_ref, out_ref):
        out_ref[0] = jnp.swapaxes(in_ref[...], 0, 1)

    return pl.pallas_call(
        body,
        grid=(4,),
        in_specs=[pl.BlockSpec((tokens, layers, part), lambda i: (0, 0, i))],
        out_specs=pl.BlockSpec((1, layers, tokens, part), lambda i: (i, 0, 0, 0)),
        out_shape=jax.ShapeDtypeStruct((4, layers, tokens, part), rows.dtype),
        compiler_params=params(),
        cost_estimate=cost(0, 4 * tokens * layers * width),
        name="pack_layers",
    )(rows)


def key_places(i, z):
    places = []
    for back in range(BACK):
        if back == 0:
            at = i
        elif back == 4:
            at = i - 1
        else:
            at = jnp.where(z < back, i - 1, i)
        places.append((back % 4, jnp.maximum(at, 0)))
    return places


def mask_bias(i, z, start_row):
    block = 4 * i + z
    inside = lax.broadcasted_iota(jnp.int32, (BLOCK, BLOCK), 0)
    query_at = block * BLOCK + lax.broadcasted_iota(jnp.int32, (BLOCK, BLOCK), 1)
    start = jnp.broadcast_to(start_row, (BLOCK, BLOCK))
    pieces = []
    for back in range(BACK):
        key_at = (block - back) * BLOCK + inside
        allowed = key_at >= start
        if back == 0:
            allowed = allowed & (key_at <= query_at)
        pieces.append(jnp.where(allowed, 0.0, MASKED).astype(f32))
    return jnp.concatenate(pieces, axis=0)


def head_rows(ref, kv):
    return jnp.concatenate(
        [
            ref[0, layer, :, pl.ds((4 * kv + head) * HD, HD)]
            for layer in range(2)
            for head in range(4)
        ],
        axis=0,
    )


def exp_scores(key_refs, places, queries, bias, kv):
    keys = jnp.concatenate(
        [key_refs[shift][at, :, pl.ds(kv * HD, HD)] for shift, at in places], axis=0
    )
    scores = lax.dot_general(keys, queries, (((1,), (1,)), ((), ())), preferred_element_type=f32)
    scores = scores * (HD**-0.5 * LOG2E) + jnp.concatenate([bias] * 8, axis=1)
    exps = jnp.exp2(scores - jnp.max(scores, axis=0, keepdims=True))
    return exps, 1.0 / jnp.sum(exps, axis=0, keepdims=True)


def value_grad_kernel(z_ref, start_ref, q_ref, g_ref, k0, k1, k2, k3, o0, o1, o2, o3, acc):
    i = pl.program_id(0)
    z = z_ref[0]

    @pl.when(i == 0)
    def _():
        acc[...] = jnp.zeros_like(acc)

    places = key_places(i, z)
    bias = mask_bias(i, z, start_ref[0])
    for kv in range(2):
        exps, inverse = exp_scores((k0, k1, k2, k3), places, head_rows(q_ref, kv), bias, kv)
        probabilities = (exps * inverse).astype(bf16)
        contrib = jnp.dot(probabilities, head_rows(g_ref, kv), preferred_element_type=f32)
        for back, (shift, at) in enumerate(places):
            acc[shift, at, :, pl.ds(kv * HD, HD)] += contrib[back * BLOCK : (back + 1) * BLOCK]

    @pl.when(i == 3)
    def _():
        for shift, out in enumerate((o0, o1, o2, o3)):
            out[...] = acc[shift].astype(bf16)


def attention_kernel(z_ref, start_ref, q_ref, k0, k1, k2, k3, v0, v1, v2, v3, out_ref):
    i = pl.program_id(0)
    z = z_ref[0]
    places = key_places(i, z)
    bias = mask_bias(i, z, start_ref[0])
    for kv in range(2):
        exps, inverse = exp_scores((k0, k1, k2, k3), places, head_rows(q_ref, kv), bias, kv)
        values = jnp.concatenate(
            [
                ref[at, :, pl.ds(kv * HD, HD)]
                for (shift, at) in places
                for ref in ((v0, v1, v2, v3)[shift],)
            ],
            axis=0,
        )
        mixed = lax.dot_general(
            values, exps.astype(bf16), (((0,), (0,)), ((), ())), preferred_element_type=f32
        )
        mixed = mixed * inverse
        for layer in range(2):
            for head in range(4):
                at = (4 * layer + head) * BLOCK
                out_ref[2 * kv + head // 2, layer, 0, :, pl.ds((head % 2) * HD, HD)] = (
                    mixed[:, at : at + BLOCK].T.astype(bf16)
                )


def attention_specs():
    whole = pl.BlockSpec((4, BLOCK, 2 * HD), lambda i, z: (0, 0, 0))
    start = pl.BlockSpec((1, 1, BLOCK), lambda i, z: (4 * i + z[0], 0, 0))
    heads = pl.BlockSpec((1, 2, BLOCK, 8 * HD), lambda i, z: (i, 0, 0, 0))
    return whole, start, heads


SCORES = 8 * BACK * BLOCK * 8 * BLOCK


def value_grad_parts(z, start, queries, cotangent, keys):
    whole, start_spec, heads = attention_specs()
    part = jax.ShapeDtypeStruct((4, BLOCK, 2 * HD), bf16)
    return pl.pallas_call(
        value_grad_kernel,
        grid_spec=pltpu.PrefetchScalarGridSpec(
            num_scalar_prefetch=1,
            grid=(4,),
            in_specs=[start_spec, heads, heads] + [whole] * 4,
            out_specs=[whole] * 4,
            scratch_shapes=[pltpu.VMEM((4, 4, BLOCK, 2 * HD), f32)],
        ),
        out_shape=[part] * 4,
        compiler_params=params(),
        cost_estimate=cost(4 * HD * SCORES, 6 << 20, SCORES),
        name="value_grad_parts",
    )(z, start, queries, cotangent, *keys)


def attend(z, start, queries, keys, values):
    whole, start_spec, heads = attention_specs()
    return pl.pallas_call(
        attention_kernel,
        grid_spec=pltpu.PrefetchScalarGridSpec(
            num_scalar_prefetch=1,
            grid=(4,),
            in_specs=[start_spec, heads] + [whole] * 8,
            out_specs=pl.BlockSpec((4, 2, 1, BLOCK, 2 * HD), lambda i, z: (0, 0, i, 0, 0)),
        ),
        out_shape=jax.ShapeDtypeStruct((4, 2, 4, BLOCK, 2 * HD), bf16),
        compiler_params=params(),
        cost_estimate=cost(4 * HD * SCORES, 6 << 20, SCORES),
        name="attend",
    )(z, start, queries, *keys, *values)


def value_parts_kernel(at_ref, h_ref, w_ref, a1, a2, a3, b1, b2, b3, out_ref, w_all):
    z = at_ref[0]
    core = at_ref[1]
    half = w_ref.shape[0] // 2
    w_all[pl.ds(pl.multiple_of(z * 2 * half, 16), 2 * half), :] = w_ref[...]
    for shift, (mine, other) in enumerate(((a1, b1), (a2, b2), (a3, b3)), 1):
        base = lax.rem(z + 4 - shift, 4) * 2 * half
        w_all[pl.ds(pl.multiple_of(base + core * half, 16), half), :] = mine[...]
        w_all[pl.ds(pl.multiple_of(base + (1 - core) * half, 16), half), :] = other[...]
    part = jnp.dot(h_ref[...], w_all[...], preferred_element_type=f32)
    out_ref[0] = (part * D**-0.5).astype(bf16)


def value_parts(place, features, weight_rows, mine, other):
    tokens = features.shape[0]
    rows, channels = weight_rows.shape
    piece = pl.BlockSpec((rows // 2, 256), lambda n, at: (0, n))
    return pl.pallas_call(
        value_parts_kernel,
        grid_spec=pltpu.PrefetchScalarGridSpec(
            num_scalar_prefetch=1,
            grid=(channels // 256,),
            in_specs=[
                pl.BlockSpec((tokens, FEATS), lambda n, at: (0, 0)),
                pl.BlockSpec((rows, 256), lambda n, at: (0, n)),
            ]
            + [piece] * 6,
            out_specs=pl.BlockSpec((1, tokens, 256), lambda n, at: (n, 0, 0)),
            scratch_shapes=[pltpu.VMEM((FEATS, 256), bf16)],
        ),
        out_shape=jax.ShapeDtypeStruct((channels // 256, tokens, 256), bf16),
        compiler_params=params(),
        cost_estimate=cost(2 * tokens * FEATS * channels, 7 << 20),
        name="value_parts",
    )(place, features, weight_rows, *mine, *other)


def sum_transposed(pieces):
    def body(p0, p1, p2, p3, out_ref):
        for block in range(4):
            total = (p0[block].astype(f32) + p1[block].astype(f32)) + (
                p2[block].astype(f32) + p3[block].astype(f32)
            )
            out_ref[:, pl.ds(block * BLOCK, BLOCK)] = total.T.astype(bf16)

    return pl.pallas_call(
        body,
        out_shape=jax.ShapeDtypeStruct((2 * HD, 4 * BLOCK), bf16),
        compiler_params=params(),
        cost_estimate=cost(1 << 19, 5 << 18),
        name="sum_transposed",
    )(*pieces)


def gradient_kernel(at_ref, g0, g1, g2, g3, h_ref, keep_ref, send_ref):
    x = at_ref[2]
    low = at_ref[1] == 0
    features = h_ref[...]
    for shift, piece in enumerate((g0, g1, g2, g3)):
        owner = lax.rem(x + 4 - shift, 4)
        part = jnp.dot(piece[...], features, preferred_element_type=f32) * D**-0.5
        for pair in range(2):
            first = part[pair * 128 : pair * 128 + 64].astype(bf16)
            second = part[pair * 128 + 64 : pair * 128 + 128].astype(bf16)
            y = 2 * lax.rem(owner, 2) + pair
            keep_ref[y, owner // 2] = jnp.where(low, first, second)
            send_ref[y, owner // 2] = jnp.where(low, second, first)


def gradient_parts(place, pieces, features):
    tokens = features.shape[0]
    piece = pl.BlockSpec((2 * HD, tokens), lambda n, at: (0, 0))
    out = pl.BlockSpec((4, 2, 64, 256), lambda n, at: (0, 0, 0, n))
    shape = jax.ShapeDtypeStruct((4, 2, 64, FEATS), bf16)
    return pl.pallas_call(
        gradient_kernel,
        grid_spec=pltpu.PrefetchScalarGridSpec(
            num_scalar_prefetch=1,
            grid=(FEATS // 256,),
            in_specs=[piece] * 4 + [pl.BlockSpec((tokens, 256), lambda n, at: (0, n))],
            out_specs=[out, out],
        ),
        out_shape=[shape, shape],
        compiler_params=params(),
        cost_estimate=cost(2 * tokens * FEATS * 1024, 7 << 20),
        name="gradient_parts",
    )(place, *pieces, features)


def sum_and_split(parts):
    width = FEATS // 4

    def body(in_ref, out_ref):
        for zh in range(2):
            total = (in_ref[0, zh].astype(f32) + in_ref[1, zh].astype(f32)) + (
                in_ref[2, zh].astype(f32) + in_ref[3, zh].astype(f32)
            )
            for z in range(4):
                out_ref[4 * zh + z] = total[:, z * width : (z + 1) * width].astype(bf16)

    return pl.pallas_call(
        body,
        out_shape=jax.ShapeDtypeStruct((8, 64, width), bf16),
        compiler_params=params(),
        cost_estimate=cost(1 << 20, 5 << 19),
        name="sum_and_split",
    )(parts)


def join_cores(place, mine, other):
    count, rows, width = mine.shape

    def body(at_ref, mine_ref, other_ref, out_ref):
        low = at_ref[1] == 0
        for at in range(count):
            a = mine_ref[at].astype(f32)
            b = other_ref[at].astype(f32)
            both = jnp.concatenate([jnp.where(low, a, b), jnp.where(low, b, a)], axis=0)
            out_ref[:, pl.ds(at * 2 * rows, 2 * rows)] = both.T.astype(bf16)

    whole = pl.BlockSpec(mine.shape, lambda at: (0, 0, 0))
    return pl.pallas_call(
        body,
        grid_spec=pltpu.PrefetchScalarGridSpec(
            num_scalar_prefetch=1,
            grid=(),
            in_specs=[whole, whole],
            out_specs=pl.BlockSpec((width, 2 * count * rows), lambda at: (0, 0)),
        ),
        out_shape=jax.ShapeDtypeStruct((width, 2 * count * rows), bf16),
        compiler_params=params(),
        cost_estimate=cost(0, 2 << 20),
        name="join_cores",
    )(place, mine, other)


def exchange(parts, axes):
    return lax.all_to_all(parts, axes, split_axis=0, concat_axis=0, tiled=True)


def from_lower(array, axis, shift):
    return lax.ppermute(array, axis, [(i, (i + shift) % 4) for i in range(4)])


def swap_cores(array):
    return lax.ppermute(array, "core", [(0, 1), (1, 0)])


def per_device(
    hidden, queries, keys, cotangent, segments, weight, master, first_moment, second_moment
):
    x, z, core = lax.axis_index("x"), lax.axis_index("z"), lax.axis_index("core")
    place = jnp.stack([z, core, x]).astype(jnp.int32)

    own_keys = exchange(pack_columns(keys[0]), "x")
    own_queries = exchange(pack_layers(queries[0]), "x")
    own_cotangent = exchange(pack_layers(cotangent[0]), "x")
    own_features = exchange(pack_columns(hidden[0]), "x").reshape(4 * BLOCK, FEATS)
    all_keys = [own_keys] + [from_lower(own_keys, "z", shift) for shift in (1, 2, 3)]

    weight_rows = weight.T
    half = weight_rows.shape[0] // 2
    own_half = lax.dynamic_slice_in_dim(weight_rows, core * half, half, 0)
    mine = [from_lower(own_half, "z", shift) for shift in (1, 2, 3)]
    other = [swap_cores(piece) for piece in mine]

    documents = jnp.arange(8, dtype=jnp.int32)
    first_of = jnp.sum((segments[0][None, :] < documents[:, None]).astype(jnp.int32), axis=1)
    start = jnp.sum(
        jnp.where(segments[0][None, :] == documents[:, None], first_of[:, None], 0), axis=0
    ).reshape(16, 1, BLOCK)

    grad_parts = value_grad_parts(place, start, own_queries, own_cotangent, all_keys)
    grad_rows = sum_transposed(
        [grad_parts[0]] + [from_lower(grad_parts[shift], "z", -shift) for shift in (1, 2, 3)]
    )
    pieces = [grad_rows] + [from_lower(grad_rows, "x", shift) for shift in (1, 2, 3)]
    keep, send = gradient_parts(place, pieces, own_features)
    both = (keep.astype(f32) + swap_cores(send).astype(f32)).astype(bf16)
    by_feature = exchange(sum_and_split(exchange(both, "y")), ("zh", "z"))
    gradient = jnp.sum(by_feature.astype(f32), axis=0)
    new_master, new_first, new_second = adam_update(gradient, master, first_moment, second_moment)
    shard = new_master.astype(bf16)
    shards = exchange(jnp.broadcast_to(shard[None], (8,) + shard.shape), ("zh", "y"))
    fresh = join_cores(place, shards, swap_cores(shards)).T

    parts = exchange(value_parts(place, own_features, weight_rows, mine, other), "x")
    own_values = jnp.sum(parts.astype(f32), axis=0).astype(bf16).reshape(4, BLOCK, 2 * HD)
    all_values = [own_values] + [from_lower(own_values, "z", shift) for shift in (1, 2, 3)]
    mixed = exchange(attend(place, start, own_queries, all_keys, all_values), "z")
    attention = mixed.transpose(1, 2, 0, 3, 4).reshape(1, 2, 16 * BLOCK, 2 * HD)
    return (attention, new_master, new_first, new_second, fresh)


def solution(mesh):
    fine = Mesh(mesh.devices.reshape(2, 4, 2, 4, 4), DP + SEQ)
    in_specs = (
        P(DP, SEQ, None),
        P(DP, SEQ, None, None),
        P(DP, SEQ, None),
        P(DP, SEQ, None, None),
        P(DP, None),
        P(None, SEQ),
        P(DP, SEQ),
        P(DP, SEQ),
        P(DP, SEQ),
    )
    out_specs = (
        P(DP, None, None, SEQ),
        P(DP, SEQ),
        P(DP, SEQ),
        P(DP, SEQ),
        P(None, SEQ),
    )
    return jax.shard_map(
        per_device, mesh=fine, in_specs=in_specs, out_specs=out_specs, check_vma=False
    )
```

```python
import jax
import jax.numpy as jnp
from jax import lax
from jax.experimental import pallas as pl
from jax.experimental.pallas import tpu as pltpu
from jax.sharding import Mesh, PartitionSpec as P

D = 7168
KVH = 8
HD = 128
BLOCK = 128
BACK = 5
FEATS = D // 4
LOG2E = 1.4426950408889634
MASKED = -1e30
VMEM_LIMIT = 32 * 1024 * 1024

beta_one = 0.9
beta_two = 0.95
rate = 0.05
stability_offset = 1e-08
first_fix = 1.0 - 0.9**20
second_fix = 1.0 - 0.95**20

bf16 = jnp.bfloat16
f32 = jnp.float32
DP = ("zh", "y", "core")
SEQ = ("x", "z")


def adam_update(gradient, master, first_moment, second_moment):
    new_first = beta_one * first_moment + (1.0 - beta_one) * gradient
    new_second = beta_two * second_moment + (1.0 - beta_two) * gradient * gradient
    step_size = new_first / first_fix / (jnp.sqrt(new_second / second_fix) + stability_offset)
    new_master = master - rate * step_size
    return (new_master, new_first, new_second)


def params(**more):
    return pltpu.CompilerParams(vmem_limit_bytes=VMEM_LIMIT, **more)


def cost(flops, nbytes, exps=0):
    return pl.CostEstimate(flops=flops, bytes_accessed=nbytes, transcendentals=exps)


def corner(array):
    shape = (1,) * (array.ndim - 2) + (16, 128)
    return pl.BlockSpec(shape, lambda *at: (0,) * array.ndim)


def call(
    body, place, arrays, in_specs, out_specs, out_shape, grid, estimate, name, scratch=(), after=()
):
    count = len(arrays)

    def kernel(at_ref, *refs):
        body(at_ref, *refs[:count], *refs[count + len(after) :])

    return pl.pallas_call(
        kernel,
        grid_spec=pltpu.PrefetchScalarGridSpec(
            num_scalar_prefetch=1,
            grid=grid,
            in_specs=list(in_specs) + [corner(array) for array in after],
            out_specs=out_specs,
            scratch_shapes=list(scratch),
        ),
        out_shape=out_shape,
        compiler_params=params(),
        cost_estimate=estimate,
        name=name,
    )(place, *arrays, *after)


def pack_columns(place, rows, after=()):
    tokens, width = rows.shape
    part = width // 4

    def body(at_ref, in_ref, out_ref):
        out_ref[0] = in_ref[...]

    return call(
        body,
        place,
        [rows],
        [pl.BlockSpec((tokens, part), lambda i, at: (0, i))],
        pl.BlockSpec((1, tokens, part), lambda i, at: (i, 0, 0)),
        jax.ShapeDtypeStruct((4, tokens, part), rows.dtype),
        (4,),
        cost(0, 4 * tokens * width),
        "pack_columns",
        after=after,
    )


def pack_layers(first, second):
    tokens, layers, width = first.shape
    part = width // 4

    def body(first_ref, second_ref, out_ref):
        out_ref[0, 0] = jnp.swapaxes(first_ref[...], 0, 1)
        out_ref[0, 1] = jnp.swapaxes(second_ref[...], 0, 1)

    piece = pl.BlockSpec((tokens, layers, part), lambda i: (0, 0, i))
    return pl.pallas_call(
        body,
        grid=(4,),
        in_specs=[piece, piece],
        out_specs=pl.BlockSpec((1, 2, layers, tokens, part), lambda i: (i, 0, 0, 0, 0)),
        out_shape=jax.ShapeDtypeStruct((4, 2, layers, tokens, part), first.dtype),
        compiler_params=pltpu.CompilerParams(vmem_limit_bytes=60 * 1024 * 1024),
        cost_estimate=cost(0, 8 * tokens * layers * width),
        name="pack_layers",
    )(first, second)


def own_quarter(place, rows, after=()):
    count, width = rows.shape

    def body(at_ref, in_ref, out_ref):
        out_ref[...] = in_ref[...]

    return call(
        body,
        place,
        [rows],
        [pl.BlockSpec((count // 4, width), lambda i, at: (2 * at[1] + at[3], 0))],
        pl.BlockSpec((count // 4, width), lambda i, at: (0, 0)),
        jax.ShapeDtypeStruct((count // 4, width), rows.dtype),
        (1,),
        cost(0, count * width),
        "own_quarter",
        after=after,
    )


def stack(place, arrays, after=()):
    shape = arrays[0].shape
    zeros = (0,) * len(shape)

    def body(at_ref, *refs):
        *in_refs, out_ref = refs
        for i, ref in enumerate(in_refs):
            out_ref[i] = ref[...]

    return call(
        body,
        place,
        arrays,
        [pl.BlockSpec(shape, lambda i, at: zeros)] * len(arrays),
        pl.BlockSpec((len(arrays),) + shape, lambda i, at: (0,) + zeros),
        jax.ShapeDtypeStruct((len(arrays),) + shape, arrays[0].dtype),
        (1,),
        cost(0, 4 * len(arrays) * arrays[0].size),
        "stack",
        after=after,
    )


def key_places(i, z, shift):
    own = lax.rem(z + 4 - shift, 4)
    places = []
    for back in range(BACK):
        if back == 0:
            at = i
        elif back == 4:
            at = i - 1
        else:
            at = jnp.where(own < back, i - 1, i)
        places.append(((shift + back) % 4, jnp.maximum(at, 0)))
    return own, places


def mask_bias(i, z, start_row):
    block = 4 * i + z
    inside = lax.broadcasted_iota(jnp.int32, (BLOCK, BLOCK), 0)
    query_at = block * BLOCK + lax.broadcasted_iota(jnp.int32, (BLOCK, BLOCK), 1)
    start = jnp.broadcast_to(start_row, (BLOCK, BLOCK))
    pieces = []
    for back in range(BACK):
        key_at = (block - back) * BLOCK + inside
        allowed = key_at >= start
        if back == 0:
            allowed = allowed & (key_at <= query_at)
        pieces.append(jnp.where(allowed, 0.0, MASKED).astype(f32))
    return jnp.concatenate(pieces, axis=0)


def head_rows(ref, kv):
    return jnp.concatenate(
        [
            ref[0, 0, layer, :, pl.ds((4 * kv + head) * HD, HD)]
            for layer in range(2)
            for head in range(4)
        ],
        axis=0,
    )


def exp_scores(keys, queries, bias):
    scores = lax.dot_general(keys, queries, (((1,), (1,)), ((), ())), preferred_element_type=f32)
    copies = queries.shape[0] // BLOCK
    scores = scores * (HD**-0.5 * LOG2E) + jnp.concatenate([bias] * copies, axis=1)
    exps = jnp.exp2(scores - jnp.max(scores, axis=0, keepdims=True))
    return exps, 1.0 / jnp.sum(exps, axis=0, keepdims=True)


def value_grad_kernel(
    at_ref, start_ref, q_ref, g_ref, key_ref, out_ref, head_ref, acc
):
    i = pl.program_id(0)
    z = at_ref[0]

    @pl.when(i == 0)
    def _():
        acc[...] = jnp.zeros_like(acc)

    own, places = key_places(i, z, 0)
    bias = mask_bias(i, own, start_ref[4 * i + own])
    for kv in range(2):
        keys = jnp.concatenate(
            [key_ref[held, at, :, pl.ds(kv * HD, HD)] for held, at in places], axis=0
        )
        exps, inverse = exp_scores(keys, head_rows(q_ref, kv), bias)
        probabilities = (exps * inverse).astype(bf16)
        contrib = jnp.dot(probabilities, head_rows(g_ref, kv), preferred_element_type=f32)
        for back, (held, at) in enumerate(places):
            acc[held, at, :, pl.ds(kv * HD, HD)] += contrib[back * BLOCK : (back + 1) * BLOCK]

    @pl.when(i == 3)
    def _():
        for held in range(4):
            out_ref[lax.rem(z + 4 - held, 4)] = acc[held].astype(bf16)
        head_ref[...] = key_ref[:, :, :, pl.ds(pl.multiple_of((z // 2) * HD, HD), HD)]


def attention_kernel(
    at_ref, start_ref, q0, q1, q2, q3, key_ref, v0, v1, v2, v3, out_ref
):
    i = pl.program_id(0)
    z = at_ref[0]
    for shift, q_ref in enumerate((q0, q1, q2, q3)):
        own, places = key_places(i, z, shift)
        bias = mask_bias(i, own, start_ref[4 * i + own])
        keys = jnp.concatenate([key_ref[held, at] for held, at in places], axis=0)
        values = jnp.concatenate([(v0, v1, v2, v3)[held][at] for held, at in places], axis=0)
        queries = jnp.concatenate(
            [
                (q_ref[0, 0] if shift == 0 else q_ref[0])[layer, :, head * HD : (head + 1) * HD]
                for layer in range(2)
                for head in range(2)
            ],
            axis=0,
        )
        exps, inverse = exp_scores(keys, queries, bias)
        mixed = lax.dot_general(
            values, exps.astype(bf16), (((0,), (0,)), ((), ())), preferred_element_type=f32
        )
        mixed = mixed * inverse
        for layer in range(2):
            for head in range(2):
                at = (2 * layer + head) * BLOCK
                out_ref[layer, 0, own, :, pl.ds(head * HD, HD)] = (
                    mixed[:, at : at + BLOCK].T.astype(bf16)
                )


SCORES = 8 * BACK * BLOCK * 8 * BLOCK
STARTS = pl.BlockSpec((16, 1, BLOCK), lambda i, at: (0, 0, 0))


def value_grad_parts(place, start, heads_and_grads, keys):
    whole = pl.BlockSpec((4, 4, BLOCK, 2 * HD), lambda i, at: (0, 0, 0, 0))
    heads = [
        pl.BlockSpec((1, 1, 2, BLOCK, 8 * HD), lambda i, at, which=which: (i, which, 0, 0, 0))
        for which in range(2)
    ]
    return call(
        value_grad_kernel,
        place,
        [start, heads_and_grads, heads_and_grads, keys],
        [STARTS] + heads + [whole],
        [whole, pl.BlockSpec((4, 4, BLOCK, HD), lambda i, at: (0, 0, 0, 0))],
        [
            jax.ShapeDtypeStruct((4, 4, BLOCK, 2 * HD), bf16),
            jax.ShapeDtypeStruct((4, 4, BLOCK, HD), bf16),
        ],
        (4,),
        cost(4 * HD * SCORES, 6 << 20, SCORES),
        "value_grad_parts",
        scratch=[pltpu.VMEM((4, 4, BLOCK, 2 * HD), f32)],
    )


def split_queries(place, heads_and_grads, hidden, after=()):
    def body(at_ref, in_ref, hidden_ref, *out_refs):
        *head_refs, features_ref = out_refs
        for shift, out in enumerate(head_refs, 1):
            pair = lax.rem(at_ref[0] + shift, 4)
            out[0] = in_ref[0, 0, :, :, pl.ds(pl.multiple_of(pair * 2 * HD, 2 * HD), 2 * HD)]
        features_ref[0] = hidden_ref[...]

    piece = pl.BlockSpec((1, 2, BLOCK, 2 * HD), lambda i, at: (i, 0, 0, 0))
    return call(
        body,
        place,
        [heads_and_grads, hidden],
        [
            pl.BlockSpec((1, 1, 2, BLOCK, 8 * HD), lambda i, at: (i, 0, 0, 0, 0)),
            pl.BlockSpec((BLOCK, FEATS), lambda i, at: (0, i)),
        ],
        [piece] * 3 + [pl.BlockSpec((1, BLOCK, FEATS), lambda i, at: (i, 0, 0))],
        [jax.ShapeDtypeStruct((4, 2, BLOCK, 2 * HD), bf16)] * 3
        + [jax.ShapeDtypeStruct((4, BLOCK, FEATS), bf16)],
        (4,),
        cost(0, 8 << 20),
        "split_queries",
        after=after,
    )


def attend(place, start, queries, keys, values):
    block = pl.BlockSpec((1, 2, BLOCK, 2 * HD), lambda i, at: (i, 0, 0, 0))
    return pl.pallas_call(
        attention_kernel,
        grid_spec=pltpu.PrefetchScalarGridSpec(
            num_scalar_prefetch=1,
            grid=(4,),
            in_specs=[
                STARTS,
                pl.BlockSpec((1, 1, 2, BLOCK, 2 * HD), lambda i, at: (i, 0, 0, 0, at[0])),
            ]
            + [block] * 3
            + [pl.BlockSpec((4, 4, BLOCK, HD), lambda i, at: (0, 0, 0, 0))]
            + [pl.BlockSpec((4, BLOCK, HD), lambda i, at: (0, 0, 0))] * 4,
            out_specs=pl.BlockSpec((2, 1, 4, BLOCK, 2 * HD), lambda i, at: (0, i, 0, 0, 0)),
        ),
        out_shape=jax.ShapeDtypeStruct((2, 4, 4, BLOCK, 2 * HD), bf16),
        compiler_params=params(),
        cost_estimate=cost(4 * HD * SCORES, 6 << 20, SCORES),
        name="attend",
    )(place, start, *queries, keys, *values).reshape(1, 2, 16 * BLOCK, 2 * HD)


def value_parts_kernel(at_ref, h_ref, w_ref, mine_ref, near_ref, far_ref, *refs):
    *out_refs, w_all = refs
    z = at_ref[0]
    core = at_ref[1]
    odd = at_ref[3]
    rows = w_ref.shape[0]
    quarter = rows // 4
    w_all[pl.ds(pl.multiple_of(z * rows, 16), rows), :] = w_ref[...]
    for shift in (1, 2, 3):
        base = lax.rem(z + 4 - shift, 4) * rows
        for piece, whose in (
            (mine_ref[shift - 1], 2 * core + odd),
            (near_ref[shift - 1], 2 * core + 1 - odd),
            (far_ref[0, shift - 1], 2 * (1 - core) + odd),
            (far_ref[1, shift - 1], 2 * (1 - core) + 1 - odd),
        ):
            at = pl.multiple_of(base + whose * quarter, 16)
            w_all[pl.ds(at, quarter), :] = piece
    part = jnp.dot(h_ref[...], w_all[...], preferred_element_type=f32)
    part = (part * D**-0.5).astype(bf16)
    for shift, out in enumerate(out_refs):

        @pl.when(pl.program_id(0) == shift)
        def _():
            out[...] = part


def value_parts(place, features, weight_rows, mine, near, far, after=()):
    tokens = features.shape[0]
    rows, channels = weight_rows.shape
    piece = pl.BlockSpec((3, rows // 4, 256), lambda n, at: (0, 0, lax.rem(at[2] + n, 4)))
    return call(
        value_parts_kernel,
        place,
        [features, weight_rows, mine, near, far],
        [
            pl.BlockSpec((tokens, FEATS), lambda n, at: (0, 0)),
            pl.BlockSpec((rows, 256), lambda n, at: (0, lax.rem(at[2] + n, 4))),
            piece,
            piece,
            pl.BlockSpec((2, 3, rows // 4, 256), lambda n, at: (0, 0, 0, lax.rem(at[2] + n, 4))),
        ],
        [pl.BlockSpec((tokens, 256), lambda n, at: (0, 0))] * 4,
        [jax.ShapeDtypeStruct((tokens, 256), bf16)] * 4,
        (channels // 256,),
        cost(2 * tokens * FEATS * channels, 7 << 20),
        "value_parts",
        scratch=[pltpu.VMEM((FEATS, 256), bf16)],
        after=after,
    )


def sum_values(place, parts):
    tokens = parts[0].shape[0]

    def body(at_ref, p0, p1, p2, p3, *out_refs):
        total = (p0[...].astype(f32) + p1[...].astype(f32)) + (
            p2[...].astype(f32) + p3[...].astype(f32)
        )
        total = total.astype(bf16).reshape(4, BLOCK, 2 * HD)
        for shift, out in enumerate(out_refs):
            low = lax.rem(at_ref[0] + shift, 4) < 2
            out[...] = jnp.where(low, total[:, :, :HD], total[:, :, HD:])

    piece = pl.BlockSpec((4, BLOCK, HD), lambda i, at: (0, 0, 0))
    return pl.pallas_call(
        body,
        grid_spec=pltpu.PrefetchScalarGridSpec(
            num_scalar_prefetch=1,
            grid=(1,),
            in_specs=[pl.BlockSpec((tokens, 2 * HD), lambda i, at: (0, 0))] * 4,
            out_specs=[piece] * 4,
        ),
        out_shape=[jax.ShapeDtypeStruct((4, BLOCK, HD), bf16)] * 4,
        compiler_params=params(),
        cost_estimate=cost(1 << 19, 3 << 19),
        name="sum_values",
    )(place, *parts)


def sum_transposed(place, parts, after=()):
    def body(at_ref, in_ref, out_ref):
        for block in range(4):
            total = (in_ref[0, block].astype(f32) + in_ref[1, block].astype(f32)) + (
                in_ref[2, block].astype(f32) + in_ref[3, block].astype(f32)
            )
            out_ref[:, block * BLOCK : (block + 1) * BLOCK] = total.T.astype(bf16)

    return call(
        body,
        place,
        [parts],
        [pl.BlockSpec((4, 4, BLOCK, 2 * HD), lambda i, at: (0, 0, 0, 0))],
        pl.BlockSpec((2 * HD, 4 * BLOCK), lambda i, at: (0, 0)),
        jax.ShapeDtypeStruct((2 * HD, 4 * BLOCK), bf16),
        (1,),
        cost(1 << 19, 5 << 18),
        "sum_transposed",
        after=after,
    )


def gradient_kernel(at_ref, g0, g1, g2, g3, h_ref, keep_ref, send_ref):
    x = at_ref[2]
    low = at_ref[1] == 0
    features = h_ref[...]
    for shift, piece in enumerate((g0, g1, g2, g3)):
        owner = lax.rem(x + 4 - shift, 4)
        part = jnp.dot(piece[...], features, preferred_element_type=f32) * D**-0.5
        for pair in range(2):
            first = part[pair * 128 : pair * 128 + 64].astype(bf16)
            second = part[pair * 128 + 64 : pair * 128 + 128].astype(bf16)
            y = 2 * lax.rem(owner, 2) + pair
            keep_ref[y, owner // 2] = jnp.where(low, first, second)
            send_ref[y, owner // 2] = jnp.where(low, second, first)


def gradient_parts(place, pieces, features, after=()):
    tokens = features.shape[0]
    out = pl.BlockSpec((4, 2, 64, 256), lambda n, at: (0, 0, 0, n))
    return call(
        gradient_kernel,
        place,
        [*pieces, features],
        [pl.BlockSpec((2 * HD, tokens), lambda n, at: (0, 0))] * 4
        + [pl.BlockSpec((tokens, 256), lambda n, at: (0, n))],
        [out, out],
        [jax.ShapeDtypeStruct((4, 2, 64, FEATS), bf16)] * 2,
        (FEATS // 256,),
        cost(2 * tokens * FEATS * 1024, 7 << 20),
        "gradient_parts",
        after=after,
    )


def add(place, first, second, after=()):
    shape = first.shape
    block = pl.BlockSpec((1,) + shape[1:], lambda i, at: (i,) + (0,) * (len(shape) - 1))

    def body(at_ref, first_ref, second_ref, out_ref):
        total = first_ref[...].astype(f32) + second_ref[...].astype(f32)
        out_ref[...] = total.astype(bf16)

    return call(
        body,
        place,
        [first, second],
        [block, block],
        block,
        jax.ShapeDtypeStruct(shape, bf16),
        (shape[0],),
        cost(first.size, 6 * first.size),
        "add",
        after=after,
    )


def sum_and_split(place, parts, after=()):
    width = FEATS // 4

    def body(at_ref, in_ref, out_ref):
        total = (in_ref[0, 0].astype(f32) + in_ref[1, 0].astype(f32)) + (
            in_ref[2, 0].astype(f32) + in_ref[3, 0].astype(f32)
        )
        for z in range(4):
            out_ref[z] = total[:, z * width : (z + 1) * width].astype(bf16)

    return call(
        body,
        place,
        [parts],
        [pl.BlockSpec((4, 1, 64, FEATS), lambda i, at: (0, i, 0, 0))],
        pl.BlockSpec((4, 64, width), lambda i, at: (i, 0, 0)),
        jax.ShapeDtypeStruct((8, 64, width), bf16),
        (2,),
        cost(1 << 20, 5 << 19),
        "sum_and_split",
        after=after,
    )


def update(place, parts, master, first_moment, second_moment, after=()):
    rows, width = master.shape

    def body(at_ref, parts_ref, master_ref, first_ref, second_ref, m_out, a_out, b_out, w_out):
        gradient = parts_ref[0].astype(f32)
        for i in range(1, 8):
            gradient = gradient + parts_ref[i].astype(f32)
        new_master, new_first, new_second = adam_update(
            gradient, master_ref[...], first_ref[...], second_ref[...]
        )
        m_out[...] = new_master
        a_out[...] = new_first
        b_out[...] = new_second
        for i in range(8):
            w_out[i] = new_master.astype(bf16)

    state = pl.BlockSpec((rows, width), lambda i, at: (0, 0))
    eight = pl.BlockSpec((8, rows, width), lambda i, at: (0, 0, 0))
    return call(
        body,
        place,
        [parts, master, first_moment, second_moment],
        [eight, state, state, state],
        [state, state, state, eight],
        [jax.ShapeDtypeStruct((rows, width), f32)] * 3
        + [jax.ShapeDtypeStruct((8, rows, width), bf16)],
        (1,),
        cost(1 << 20, 2 << 20),
        "update",
        after=after,
    )


def join_cores(place, mine, other):
    count, rows, width = mine.shape

    def body(at_ref, mine_ref, other_ref, out_ref):
        low = at_ref[1] == 0
        for at in range(count):
            a = mine_ref[at].astype(f32)
            b = other_ref[at].astype(f32)
            both = jnp.concatenate([jnp.where(low, a, b), jnp.where(low, b, a)], axis=0)
            out_ref[:, pl.ds(at * 2 * rows, 2 * rows)] = both.T.astype(bf16)

    whole = pl.BlockSpec(mine.shape, lambda at: (0, 0, 0))
    return pl.pallas_call(
        body,
        grid_spec=pltpu.PrefetchScalarGridSpec(
            num_scalar_prefetch=1,
            grid=(),
            in_specs=[whole, whole],
            out_specs=pl.BlockSpec((width, 2 * count * rows), lambda at: (0, 0)),
        ),
        out_shape=jax.ShapeDtypeStruct((width, 2 * count * rows), bf16),
        compiler_params=params(),
        cost_estimate=cost(0, 2 << 20),
        name="join_cores",
    )(place, mine, other)


def exchange(parts, axes):
    return lax.all_to_all(parts, axes, split_axis=0, concat_axis=0, tiled=True)


def from_lower(array, axis, shift):
    return lax.ppermute(array, axis, [(i, (i + shift) % 4) for i in range(4)])


def swap_cores(array):
    return lax.ppermute(array, "core", [(0, 1), (1, 0)])


def per_device(
    hidden, queries, keys, cotangent, segments, weight, master, first_moment, second_moment
):
    x, y, z, core = (lax.axis_index(name) for name in ("x", "y", "z", "core"))
    odd = lax.rem(y, 2)
    place = jnp.stack([z, core, x, odd]).astype(jnp.int32)

    documents = jnp.arange(8, dtype=jnp.int32)
    first_of = jnp.sum((segments[0][None, :] < documents[:, None]).astype(jnp.int32), axis=1)
    start = jnp.sum(
        jnp.where(segments[0][None, :] == documents[:, None], first_of[:, None], 0), axis=0
    ).reshape(16, 1, BLOCK)

    own_keys = exchange(pack_columns(place, keys[0]), "x")
    packed = pack_layers(queries[0], cotangent[0])
    heads_and_grads = exchange(packed, "x")
    all_keys = stack(
        place, [own_keys] + [from_lower(own_keys, "z", shift) for shift in (1, 2, 3)]
    )

    weight_rows = weight.T
    sent_quarter = own_quarter(place, weight_rows, after=[own_keys])
    mine = stack(place, [from_lower(sent_quarter, "z", shift) for shift in (1, 2, 3)])

    *queries_to, features_to = split_queries(
        place, heads_and_grads, hidden[0], after=[mine, all_keys]
    )
    own_features = exchange(features_to, "x").reshape(4 * BLOCK, FEATS)
    queries_from = [heads_and_grads] + [
        from_lower(piece, "z", shift) for shift, piece in enumerate(queries_to, 1)
    ]

    grad_parts, key_heads = value_grad_parts(place, start, heads_and_grads, all_keys)
    grad_moved = exchange(grad_parts, "z")

    near = lax.ppermute(mine, "y", [(0, 1), (1, 0), (2, 3), (3, 2)])
    ready = [grad_parts, queries_from[1], queries_from[3]]
    far = swap_cores(stack(place, [mine, near], after=ready))
    parts_to = value_parts(place, own_features, weight_rows, mine, near, far)
    parts_from = [parts_to[0]] + [from_lower(parts_to[shift], "x", shift) for shift in (1, 2, 3)]
    values = sum_values(place, parts_from)
    values_from = [values[0]] + [from_lower(values[shift], "z", shift) for shift in (1, 2, 3)]

    grad_rows = sum_transposed(place, grad_moved, after=[values[0]])
    pieces = [grad_rows] + [from_lower(grad_rows, "x", shift) for shift in (1, 2, 3)]
    keep, send = gradient_parts(place, pieces, own_features, after=values_from[1:])
    both = add(place, keep, swap_cores(send))
    split = sum_and_split(
        place, exchange(both, "y"), after=[queries_from[2]]
    )
    by_feature = exchange(split, ("zh", "z"))
    attention = attend(place, start, queries_from, key_heads, values_from)
    new_master, new_first, new_second, shard = update(
        place, by_feature, master, first_moment, second_moment, after=[attention]
    )
    shards = exchange(shard, ("zh", "y"))
    fresh = join_cores(place, shards, swap_cores(shards)).T
    return (attention, new_master, new_first, new_second, fresh)


def solution(mesh):
    fine = Mesh(mesh.devices.reshape(2, 4, 2, 4, 4), DP + SEQ)
    in_specs = (
        P(DP, SEQ, None),
        P(DP, SEQ, None, None),
        P(DP, SEQ, None),
        P(DP, SEQ, None, None),
        P(DP, None),
        P(None, SEQ),
        P(DP, SEQ),
        P(DP, SEQ),
        P(DP, SEQ),
    )
    out_specs = (
        P(DP, None, None, SEQ),
        P(DP, SEQ),
        P(DP, SEQ),
        P(DP, SEQ),
        P(None, SEQ),
    )
    return jax.shard_map(
        per_device, mesh=fine, in_specs=in_specs, out_specs=out_specs, check_vma=False
    )
```

```python
import jax
import jax.numpy as jnp
from jax import lax
from jax.experimental import pallas as pl
from jax.experimental.pallas import tpu as pltpu
from jax.sharding import Mesh, PartitionSpec as P

D = 7168
KVH = 8
HD = 128
BLOCK = 128
BACK = 5
FEATS = D // 4
LOG2E = 1.4426950408889634
MASKED = -1e30
VMEM_LIMIT = 32 * 1024 * 1024

beta_one = 0.9
beta_two = 0.95
rate = 0.05
stability_offset = 1e-08
first_fix = 1.0 - 0.9**20
second_fix = 1.0 - 0.95**20

bf16 = jnp.bfloat16
f32 = jnp.float32
DP = ("zh", "y", "core")
SEQ = ("x", "z")


def adam_update(gradient, master, first_moment, second_moment):
    new_first = beta_one * first_moment + (1.0 - beta_one) * gradient
    new_second = beta_two * second_moment + (1.0 - beta_two) * gradient * gradient
    step_size = new_first / first_fix / (jnp.sqrt(new_second / second_fix) + stability_offset)
    new_master = master - rate * step_size
    return (new_master, new_first, new_second)


def params(**more):
    return pltpu.CompilerParams(vmem_limit_bytes=VMEM_LIMIT, **more)


def cost(flops, nbytes, exps=0):
    return pl.CostEstimate(flops=flops, bytes_accessed=nbytes, transcendentals=exps)


def corner(array):
    shape = (1,) * (array.ndim - 2) + (16, 128)
    return pl.BlockSpec(shape, lambda *at: (0,) * array.ndim)


def call(
    body, place, arrays, in_specs, out_specs, out_shape, grid, estimate, name, scratch=(), after=()
):
    count = len(arrays)

    def kernel(at_ref, *refs):
        body(at_ref, *refs[:count], *refs[count + len(after) :])

    return pl.pallas_call(
        kernel,
        grid_spec=pltpu.PrefetchScalarGridSpec(
            num_scalar_prefetch=1,
            grid=grid,
            in_specs=list(in_specs) + [corner(array) for array in after],
            out_specs=out_specs,
            scratch_shapes=list(scratch),
        ),
        out_shape=out_shape,
        compiler_params=params(),
        cost_estimate=estimate,
        name=name,
    )(place, *arrays, *after)


def pack_columns(place, rows):
    tokens, width = rows.shape
    part = width // 4

    def body(at_ref, in_ref, out_ref):
        for i in range(4):
            out_ref[i] = in_ref[:, i * part : (i + 1) * part]

    return call(
        body,
        place,
        [rows],
        [pl.BlockSpec((tokens, width), lambda i, at: (0, 0))],
        pl.BlockSpec((4, tokens, part), lambda i, at: (0, 0, 0)),
        jax.ShapeDtypeStruct((4, tokens, part), rows.dtype),
        (1,),
        cost(0, 4 * tokens * width),
        "pack_columns",
    )


def pack_layers(first, second):
    tokens, layers, width = first.shape
    part = width // 4

    def body(first_ref, second_ref, out_ref):
        out_ref[0, 0] = jnp.swapaxes(first_ref[...], 0, 1)
        out_ref[0, 1] = jnp.swapaxes(second_ref[...], 0, 1)

    piece = pl.BlockSpec((tokens, layers, part), lambda i: (0, 0, i))
    return pl.pallas_call(
        body,
        grid=(4,),
        in_specs=[piece, piece],
        out_specs=pl.BlockSpec((1, 2, layers, tokens, part), lambda i: (i, 0, 0, 0, 0)),
        out_shape=jax.ShapeDtypeStruct((4, 2, layers, tokens, part), first.dtype),
        compiler_params=pltpu.CompilerParams(vmem_limit_bytes=60 * 1024 * 1024),
        cost_estimate=cost(0, 8 * tokens * layers * width),
        name="pack_layers",
    )(first, second)


def own_quarter(place, rows, after=()):
    count, width = rows.shape

    def body(at_ref, in_ref, out_ref):
        out_ref[...] = in_ref[...]

    return call(
        body,
        place,
        [rows],
        [pl.BlockSpec((count // 4, width), lambda i, at: (2 * at[1] + at[3], 0))],
        pl.BlockSpec((count // 4, width), lambda i, at: (0, 0)),
        jax.ShapeDtypeStruct((count // 4, width), rows.dtype),
        (1,),
        cost(0, count * width),
        "own_quarter",
        after=after,
    )


def stack(place, arrays, after=()):
    shape = arrays[0].shape
    zeros = (0,) * len(shape)

    def body(at_ref, *refs):
        *in_refs, out_ref = refs
        for i, ref in enumerate(in_refs):
            out_ref[i] = ref[...]

    return call(
        body,
        place,
        arrays,
        [pl.BlockSpec(shape, lambda i, at: zeros)] * len(arrays),
        pl.BlockSpec((len(arrays),) + shape, lambda i, at: (0,) + zeros),
        jax.ShapeDtypeStruct((len(arrays),) + shape, arrays[0].dtype),
        (1,),
        cost(0, 4 * len(arrays) * arrays[0].size),
        "stack",
        after=after,
    )


def key_places(i, z, shift):
    own = lax.rem(z + 4 - shift, 4)
    places = []
    for back in range(BACK):
        if back == 0:
            at = i
        elif back == 4:
            at = i - 1
        else:
            at = jnp.where(own < back, i - 1, i)
        places.append(((shift + back) % 4, jnp.maximum(at, 0)))
    return own, places


def mask_bias(i, z, start_row):
    block = 4 * i + z
    inside = lax.broadcasted_iota(jnp.int32, (BLOCK, BLOCK), 0)
    query_at = block * BLOCK + lax.broadcasted_iota(jnp.int32, (BLOCK, BLOCK), 1)
    start = jnp.broadcast_to(start_row, (BLOCK, BLOCK))
    pieces = []
    for back in range(BACK):
        key_at = (block - back) * BLOCK + inside
        allowed = key_at >= start
        if back == 0:
            allowed = allowed & (key_at <= query_at)
        pieces.append(jnp.where(allowed, 0.0, MASKED).astype(f32))
    return jnp.concatenate(pieces, axis=0)


def head_rows(ref, kv):
    return jnp.concatenate(
        [
            ref[0, 0, layer, :, pl.ds((4 * kv + head) * HD, HD)]
            for layer in range(2)
            for head in range(4)
        ],
        axis=0,
    )


def exp_scores(keys, queries, bias):
    scores = lax.dot_general(keys, queries, (((1,), (1,)), ((), ())), preferred_element_type=f32)
    copies = queries.shape[0] // BLOCK
    scores = scores * (HD**-0.5 * LOG2E) + jnp.concatenate([bias] * copies, axis=1)
    exps = jnp.exp2(scores - jnp.max(scores, axis=0, keepdims=True))
    return exps, 1.0 / jnp.sum(exps, axis=0, keepdims=True)


def value_grad_kernel(
    at_ref, start_ref, q_ref, g_ref, key_ref, out_ref, head_ref, acc
):
    i = pl.program_id(0)
    z = at_ref[0]

    @pl.when(i == 0)
    def _():
        acc[...] = jnp.zeros_like(acc)

    own, places = key_places(i, z, 0)
    bias = mask_bias(i, own, start_ref[4 * i + own])
    for kv in range(2):
        keys = jnp.concatenate(
            [key_ref[held, at, :, pl.ds(kv * HD, HD)] for held, at in places], axis=0
        )
        exps, inverse = exp_scores(keys, head_rows(q_ref, kv), bias)
        probabilities = (exps * inverse).astype(bf16)
        contrib = jnp.dot(probabilities, head_rows(g_ref, kv), preferred_element_type=f32)
        for back, (held, at) in enumerate(places):
            acc[held, at, :, pl.ds(kv * HD, HD)] += contrib[back * BLOCK : (back + 1) * BLOCK]

    @pl.when(i == 3)
    def _():
        for held in range(4):
            out_ref[lax.rem(z + 4 - held, 4)] = acc[held].astype(bf16)
        head_ref[...] = key_ref[:, :, :, pl.ds(pl.multiple_of((z // 2) * HD, HD), HD)]


def attention_kernel(
    at_ref, start_ref, q0, q1, q2, q3, key_ref, v0, v1, v2, v3, out_ref
):
    i = pl.program_id(0)
    z = at_ref[0]
    for shift, q_ref in enumerate((q0, q1, q2, q3)):
        own, places = key_places(i, z, shift)
        bias = mask_bias(i, own, start_ref[4 * i + own])
        keys = jnp.concatenate([key_ref[held, at] for held, at in places], axis=0)
        values = jnp.concatenate([(v0, v1, v2, v3)[held][at] for held, at in places], axis=0)
        queries = jnp.concatenate(
            [
                (q_ref[0, 0] if shift == 0 else q_ref[0])[layer, :, head * HD : (head + 1) * HD]
                for layer in range(2)
                for head in range(2)
            ],
            axis=0,
        )
        exps, inverse = exp_scores(keys, queries, bias)
        mixed = lax.dot_general(
            values, exps.astype(bf16), (((0,), (0,)), ((), ())), preferred_element_type=f32
        )
        mixed = mixed * inverse
        for layer in range(2):
            for head in range(2):
                at = (2 * layer + head) * BLOCK
                out_ref[layer, 0, own, :, pl.ds(head * HD, HD)] = (
                    mixed[:, at : at + BLOCK].T.astype(bf16)
                )


SCORES = 8 * BACK * BLOCK * 8 * BLOCK
STARTS = pl.BlockSpec((16, 1, BLOCK), lambda i, at: (0, 0, 0))


def value_grad_parts(place, start, heads_and_grads, keys, after=()):
    whole = pl.BlockSpec((4, 4, BLOCK, 2 * HD), lambda i, at: (0, 0, 0, 0))
    heads = [
        pl.BlockSpec((1, 1, 2, BLOCK, 8 * HD), lambda i, at, which=which: (i, which, 0, 0, 0))
        for which in range(2)
    ]
    return call(
        value_grad_kernel,
        place,
        [start, heads_and_grads, heads_and_grads, keys],
        [STARTS] + heads + [whole],
        [whole, pl.BlockSpec((4, 4, BLOCK, HD), lambda i, at: (0, 0, 0, 0))],
        [
            jax.ShapeDtypeStruct((4, 4, BLOCK, 2 * HD), bf16),
            jax.ShapeDtypeStruct((4, 4, BLOCK, HD), bf16),
        ],
        (4,),
        cost(4 * HD * SCORES, 6 << 20, SCORES),
        "value_grad_parts",
        after=after,
        scratch=[pltpu.VMEM((4, 4, BLOCK, 2 * HD), f32)],
    )


def split_queries(place, heads_and_grads, after=()):
    def body(at_ref, in_ref, *out_refs):
        for shift, out in enumerate(out_refs, 1):
            pair = lax.rem(at_ref[0] + shift, 4)
            out[0] = in_ref[0, 0, :, :, pl.ds(pl.multiple_of(pair * 2 * HD, 2 * HD), 2 * HD)]

    piece = pl.BlockSpec((1, 2, BLOCK, 2 * HD), lambda i, at: (i, 0, 0, 0))
    return call(
        body,
        place,
        [heads_and_grads],
        [pl.BlockSpec((1, 1, 2, BLOCK, 8 * HD), lambda i, at: (i, 0, 0, 0, 0))],
        [piece] * 3,
        [jax.ShapeDtypeStruct((4, 2, BLOCK, 2 * HD), bf16)] * 3,
        (4,),
        cost(0, 4 << 20),
        "split_queries",
        after=after,
    )


def split_columns(place, rows, after=()):
    tokens, width = rows.shape
    part = width // 4

    def body(at_ref, *refs):
        for in_ref, out_ref in zip(refs[:4], refs[4:]):
            out_ref[...] = in_ref[...]

    return call(
        body,
        place,
        [rows] * 4,
        [
            pl.BlockSpec((tokens, part), lambda i, at, shift=shift: (0, lax.rem(at[2] + shift, 4)))
            for shift in range(4)
        ],
        [pl.BlockSpec((tokens, part), lambda i, at: (0, 0))] * 4,
        [jax.ShapeDtypeStruct((tokens, part), rows.dtype)] * 4,
        (1,),
        cost(0, 4 * tokens * width),
        "split_columns",
        after=after,
    )


def place_tokens(x, pieces, out_ref):
    for shift, piece in enumerate(pieces):
        at = pl.multiple_of(lax.rem(x + 4 - shift, 4) * BLOCK, BLOCK)
        out_ref[pl.ds(at, BLOCK), :] = piece[...]


def attend(place, start, queries, keys, values):
    block = pl.BlockSpec((1, 2, BLOCK, 2 * HD), lambda i, at: (i, 0, 0, 0))
    return pl.pallas_call(
        attention_kernel,
        grid_spec=pltpu.PrefetchScalarGridSpec(
            num_scalar_prefetch=1,
            grid=(4,),
            in_specs=[
                STARTS,
                pl.BlockSpec((1, 1, 2, BLOCK, 2 * HD), lambda i, at: (i, 0, 0, 0, at[0])),
            ]
            + [block] * 3
            + [pl.BlockSpec((4, 4, BLOCK, HD), lambda i, at: (0, 0, 0, 0))]
            + [pl.BlockSpec((4, BLOCK, HD), lambda i, at: (0, 0, 0))] * 4,
            out_specs=pl.BlockSpec((2, 1, 4, BLOCK, 2 * HD), lambda i, at: (0, i, 0, 0, 0)),
        ),
        out_shape=jax.ShapeDtypeStruct((2, 4, 4, BLOCK, 2 * HD), bf16),
        compiler_params=params(),
        cost_estimate=cost(4 * HD * SCORES, 6 << 20, SCORES),
        name="attend",
    )(place, start, *queries, keys, *values)


def value_parts_kernel(at_ref, h0, h1, h2, h3, w_ref, mine_ref, near_ref, far_ref, *refs):
    *out_refs, h_all, w_all = refs

    @pl.when(pl.program_id(0) == 0)
    def _():
        place_tokens(at_ref[2], (h0, h1, h2, h3), h_all)

    z = at_ref[0]
    core = at_ref[1]
    odd = at_ref[3]
    rows = w_ref.shape[0]
    quarter = rows // 4
    w_all[pl.ds(pl.multiple_of(z * rows, 16), rows), :] = w_ref[...]
    for shift in (1, 2, 3):
        base = lax.rem(z + 4 - shift, 4) * rows
        for piece, whose in (
            (mine_ref[shift - 1], 2 * core + odd),
            (near_ref[shift - 1], 2 * core + 1 - odd),
            (far_ref[0, shift - 1], 2 * (1 - core) + odd),
            (far_ref[1, shift - 1], 2 * (1 - core) + 1 - odd),
        ):
            at = pl.multiple_of(base + whose * quarter, 16)
            w_all[pl.ds(at, quarter), :] = piece
    part = jnp.dot(h_all[...], w_all[...], preferred_element_type=f32)
    part = (part * D**-0.5).astype(bf16)
    for shift, out in enumerate(out_refs):

        @pl.when(pl.program_id(0) == shift)
        def _():
            out[...] = part


def value_parts(place, features, weight_rows, mine, near, far, after=()):
    tokens = 4 * BLOCK
    rows, channels = weight_rows.shape
    piece = pl.BlockSpec((3, rows // 4, 256), lambda n, at: (0, 0, lax.rem(at[2] + n, 4)))
    return call(
        value_parts_kernel,
        place,
        [*features, weight_rows, mine, near, far],
        [pl.BlockSpec((BLOCK, FEATS), lambda n, at: (0, 0))] * 4
        + [
            pl.BlockSpec((rows, 256), lambda n, at: (0, lax.rem(at[2] + n, 4))),
            piece,
            piece,
            pl.BlockSpec((2, 3, rows // 4, 256), lambda n, at: (0, 0, 0, lax.rem(at[2] + n, 4))),
        ],
        [pl.BlockSpec((tokens, 256), lambda n, at: (0, 0))] * 4
        + [pl.BlockSpec((tokens, FEATS), lambda n, at: (0, 0))],
        [jax.ShapeDtypeStruct((tokens, 256), bf16)] * 4
        + [jax.ShapeDtypeStruct((tokens, FEATS), bf16)],
        (channels // 256,),
        cost(2 * tokens * FEATS * channels, 7 << 20),
        "value_parts",
        scratch=[pltpu.VMEM((FEATS, 256), bf16)],
        after=after,
    )


def sum_values(place, parts):
    tokens = parts[0].shape[0]

    def body(at_ref, p0, p1, p2, p3, *out_refs):
        total = (p0[...].astype(f32) + p1[...].astype(f32)) + (
            p2[...].astype(f32) + p3[...].astype(f32)
        )
        total = total.astype(bf16).reshape(4, BLOCK, 2 * HD)
        for shift, out in enumerate(out_refs):
            low = lax.rem(at_ref[0] + shift, 4) < 2
            out[...] = jnp.where(low, total[:, :, :HD], total[:, :, HD:])

    piece = pl.BlockSpec((4, BLOCK, HD), lambda i, at: (0, 0, 0))
    return pl.pallas_call(
        body,
        grid_spec=pltpu.PrefetchScalarGridSpec(
            num_scalar_prefetch=1,
            grid=(1,),
            in_specs=[pl.BlockSpec((tokens, 2 * HD), lambda i, at: (0, 0))] * 4,
            out_specs=[piece] * 4,
        ),
        out_shape=[jax.ShapeDtypeStruct((4, BLOCK, HD), bf16)] * 4,
        compiler_params=params(),
        cost_estimate=cost(1 << 19, 3 << 19),
        name="sum_values",
    )(place, *parts)


def sum_transposed(place, parts, after=()):
    def body(at_ref, in_ref, out_ref):
        for block in range(4):
            total = (in_ref[0, block].astype(f32) + in_ref[1, block].astype(f32)) + (
                in_ref[2, block].astype(f32) + in_ref[3, block].astype(f32)
            )
            out_ref[:, block * BLOCK : (block + 1) * BLOCK] = total.T.astype(bf16)

    return call(
        body,
        place,
        [parts],
        [pl.BlockSpec((4, 4, BLOCK, 2 * HD), lambda i, at: (0, 0, 0, 0))],
        pl.BlockSpec((2 * HD, 4 * BLOCK), lambda i, at: (0, 0)),
        jax.ShapeDtypeStruct((2 * HD, 4 * BLOCK), bf16),
        (1,),
        cost(1 << 19, 5 << 18),
        "sum_transposed",
        after=after,
    )


def gradient_kernel(at_ref, g0, g1, g2, g3, h_ref, keep_ref, send_ref):
    x = at_ref[2]
    low = at_ref[1] == 0
    features = h_ref[...]
    for shift, piece in enumerate((g0, g1, g2, g3)):
        owner = lax.rem(x + 4 - shift, 4)
        part = jnp.dot(piece[...], features, preferred_element_type=f32) * D**-0.5
        for pair in range(2):
            first = part[pair * 128 : pair * 128 + 64].astype(bf16)
            second = part[pair * 128 + 64 : pair * 128 + 128].astype(bf16)
            y = 2 * lax.rem(owner, 2) + pair
            keep_ref[y, owner // 2] = jnp.where(low, first, second)
            send_ref[y, owner // 2] = jnp.where(low, second, first)


def gradient_parts(place, pieces, features, after=()):
    tokens = 4 * BLOCK
    out = pl.BlockSpec((4, 2, 64, 256), lambda n, at: (0, 0, 0, n))
    return call(
        gradient_kernel,
        place,
        [*pieces, features],
        [pl.BlockSpec((2 * HD, tokens), lambda n, at: (0, 0))] * 4
        + [pl.BlockSpec((tokens, 256), lambda n, at: (0, n))],
        [out, out],
        [jax.ShapeDtypeStruct((4, 2, 64, FEATS), bf16)] * 2,
        (FEATS // 256,),
        cost(2 * tokens * FEATS * 1024, 7 << 20),
        "gradient_parts",
        after=after,
    )


def add(place, first, second, after=()):
    shape = first.shape
    block = pl.BlockSpec((1,) + shape[1:], lambda i, at: (i,) + (0,) * (len(shape) - 1))

    def body(at_ref, first_ref, second_ref, out_ref):
        total = first_ref[...].astype(f32) + second_ref[...].astype(f32)
        out_ref[...] = total.astype(bf16)

    return call(
        body,
        place,
        [first, second],
        [block, block],
        block,
        jax.ShapeDtypeStruct(shape, bf16),
        (shape[0],),
        cost(first.size, 6 * first.size),
        "add",
        after=after,
    )


def sum_and_split(place, parts, after=()):
    width = FEATS // 4

    def body(at_ref, in_ref, out_ref):
        total = (in_ref[0, 0].astype(f32) + in_ref[1, 0].astype(f32)) + (
            in_ref[2, 0].astype(f32) + in_ref[3, 0].astype(f32)
        )
        for z in range(4):
            out_ref[z] = total[:, z * width : (z + 1) * width].astype(bf16)

    return call(
        body,
        place,
        [parts],
        [pl.BlockSpec((4, 1, 64, FEATS), lambda i, at: (0, i, 0, 0))],
        pl.BlockSpec((4, 64, width), lambda i, at: (i, 0, 0)),
        jax.ShapeDtypeStruct((8, 64, width), bf16),
        (2,),
        cost(1 << 20, 5 << 19),
        "sum_and_split",
        after=after,
    )


def update(place, parts, master, first_moment, second_moment, after=()):
    rows, width = master.shape

    def body(at_ref, parts_ref, master_ref, first_ref, second_ref, m_out, a_out, b_out, w_out):
        gradient = parts_ref[0].astype(f32)
        for i in range(1, 8):
            gradient = gradient + parts_ref[i].astype(f32)
        new_master, new_first, new_second = adam_update(
            gradient, master_ref[...], first_ref[...], second_ref[...]
        )
        m_out[...] = new_master
        a_out[...] = new_first
        b_out[...] = new_second
        for i in range(8):
            w_out[i] = new_master.astype(bf16)

    state = pl.BlockSpec((rows, width), lambda i, at: (0, 0))
    eight = pl.BlockSpec((8, rows, width), lambda i, at: (0, 0, 0))
    return call(
        body,
        place,
        [parts, master, first_moment, second_moment],
        [eight, state, state, state],
        [state, state, state, eight],
        [jax.ShapeDtypeStruct((rows, width), f32)] * 3
        + [jax.ShapeDtypeStruct((8, rows, width), bf16)],
        (1,),
        cost(1 << 20, 2 << 20),
        "update",
        after=after,
    )


def join_cores(place, mine, other, after=()):
    count, rows, width = mine.shape

    def body(at_ref, mine_ref, other_ref, out_ref):
        low = at_ref[1] == 0
        for at in range(count):
            a = mine_ref[at].astype(f32)
            b = other_ref[at].astype(f32)
            both = jnp.concatenate([jnp.where(low, a, b), jnp.where(low, b, a)], axis=0)
            out_ref[:, pl.ds(at * 2 * rows, 2 * rows)] = both.T.astype(bf16)

    return call(
        body,
        place,
        [mine, other],
        [pl.BlockSpec(mine.shape, lambda i, at: (0, 0, 0))] * 2,
        pl.BlockSpec((width, 2 * count * rows), lambda i, at: (0, 0)),
        jax.ShapeDtypeStruct((width, 2 * count * rows), bf16),
        (1,),
        cost(0, 2 << 20),
        "join_cores",
        after=after,
    )


def exchange(parts, axes):
    return lax.all_to_all(parts, axes, split_axis=0, concat_axis=0, tiled=True)


def from_lower(array, axis, shift):
    return lax.ppermute(array, axis, [(i, (i + shift) % 4) for i in range(4)])


def swap_cores(array):
    return lax.ppermute(array, "core", [(0, 1), (1, 0)])


def per_device(
    hidden, queries, keys, cotangent, segments, weight, master, first_moment, second_moment
):
    x, y, z, core = (lax.axis_index(name) for name in ("x", "y", "z", "core"))
    odd = lax.rem(y, 2)
    place = jnp.stack([z, core, x, odd]).astype(jnp.int32)

    documents = jnp.arange(8, dtype=jnp.int32)
    first_of = jnp.sum((segments[0][None, :] < documents[:, None]).astype(jnp.int32), axis=1)
    start = jnp.sum(
        jnp.where(segments[0][None, :] == documents[:, None], first_of[:, None], 0), axis=0
    ).reshape(16, 1, BLOCK)

    own_keys = exchange(pack_columns(place, keys[0]), "x")
    packed = pack_layers(queries[0], cotangent[0])
    heads_and_grads = exchange(packed, "x")
    all_keys = stack(
        place, [own_keys] + [from_lower(own_keys, "z", shift) for shift in (1, 2, 3)]
    )

    weight_rows = weight.T
    sent_quarter = own_quarter(place, weight_rows, after=[own_keys])
    mine = stack(place, [from_lower(sent_quarter, "z", shift) for shift in (1, 2, 3)])

    grad_parts, key_heads = value_grad_parts(
        place, start, heads_and_grads, all_keys, after=[mine]
    )
    grad_moved = exchange(grad_parts, "z")

    features_to = split_columns(place, hidden[0], after=[grad_parts])
    own_features = [features_to[0]] + [
        from_lower(features_to[shift], "x", shift) for shift in (1, 2, 3)
    ]
    queries_to = split_queries(place, heads_and_grads, after=[grad_parts])
    queries_from = [heads_and_grads] + [
        from_lower(piece, "z", shift) for shift, piece in enumerate(queries_to, 1)
    ]

    grad_rows = sum_transposed(place, grad_moved)
    pieces = [grad_rows] + [from_lower(grad_rows, "x", shift) for shift in (1, 2, 3)]

    near = lax.ppermute(mine, "y", [(0, 1), (1, 0), (2, 3), (3, 2)])
    far = swap_cores(stack(place, [mine, near], after=[grad_parts]))
    *parts_to, all_features = value_parts(place, own_features, weight_rows, mine, near, far)
    parts_from = [parts_to[0]] + [from_lower(parts_to[shift], "x", shift) for shift in (1, 2, 3)]
    values = sum_values(place, parts_from)
    values_from = [values[0]] + [from_lower(values[shift], "z", shift) for shift in (1, 2, 3)]

    keep, send = gradient_parts(
        place, pieces, all_features, after=[queries_from[1], queries_from[3]]
    )
    both = add(place, keep, swap_cores(send))
    split = sum_and_split(
        place, exchange(both, "y"), after=[queries_from[2]] + values_from[1:]
    )
    by_feature = exchange(split, ("zh", "z"))
    attention = attend(place, start, queries_from, key_heads, values_from)
    new_master, new_first, new_second, shard = update(
        place, by_feature, master, first_moment, second_moment, after=[attention]
    )
    shards = exchange(shard, ("zh", "y"))
    fresh = join_cores(place, shards, swap_cores(shards)).T
    attention = attention.reshape(1, 2, 16 * BLOCK, 2 * HD)
    return (attention, new_master, new_first, new_second, fresh)


def solution(mesh):
    fine = Mesh(mesh.devices.reshape(2, 4, 2, 4, 4), DP + SEQ)
    in_specs = (
        P(DP, SEQ, None),
        P(DP, SEQ, None, None),
        P(DP, SEQ, None),
        P(DP, SEQ, None, None),
        P(DP, None),
        P(None, SEQ),
        P(DP, SEQ),
        P(DP, SEQ),
        P(DP, SEQ),
    )
    out_specs = (
        P(DP, None, None, SEQ),
        P(DP, SEQ),
        P(DP, SEQ),
        P(DP, SEQ),
        P(None, SEQ),
    )
    return jax.shard_map(
        per_device, mesh=fine, in_specs=in_specs, out_specs=out_specs, check_vma=False
    )
```

```python
import jax
import jax.numpy as jnp
from jax import lax
from jax.experimental import pallas as pl
from jax.experimental.pallas import tpu as pltpu
from jax.sharding import Mesh, PartitionSpec as P

D = 7168
KVH = 8
HD = 128
BLOCK = 128
BACK = 5
FEATS = D // 4
LOG2E = 1.4426950408889634
MASKED = -1e30
VMEM_LIMIT = 32 * 1024 * 1024

beta_one = 0.9
beta_two = 0.95
rate = 0.05
stability_offset = 1e-08
first_fix = 1.0 - 0.9**20
second_fix = 1.0 - 0.95**20

bf16 = jnp.bfloat16
f32 = jnp.float32
DP = ("zh", "y", "core")
SEQ = ("x", "z")


def adam_update(gradient, master, first_moment, second_moment):
    new_first = beta_one * first_moment + (1.0 - beta_one) * gradient
    new_second = beta_two * second_moment + (1.0 - beta_two) * gradient * gradient
    step_size = new_first / first_fix / (jnp.sqrt(new_second / second_fix) + stability_offset)
    new_master = master - rate * step_size
    return (new_master, new_first, new_second)


def params(**more):
    return pltpu.CompilerParams(vmem_limit_bytes=VMEM_LIMIT, **more)


def cost(flops, nbytes, exps=0):
    return pl.CostEstimate(flops=flops, bytes_accessed=nbytes, transcendentals=exps)


def corner(array):
    shape = (1,) * (array.ndim - 2) + (16, 128)
    return pl.BlockSpec(shape, lambda *at: (0,) * array.ndim)


def call(
    body, place, arrays, in_specs, out_specs, out_shape, grid, estimate, name, scratch=(), after=()
):
    count = len(arrays)

    def kernel(at_ref, *refs):
        body(at_ref, *refs[:count], *refs[count + len(after) :])

    return pl.pallas_call(
        kernel,
        grid_spec=pltpu.PrefetchScalarGridSpec(
            num_scalar_prefetch=1,
            grid=grid,
            in_specs=list(in_specs) + [corner(array) for array in after],
            out_specs=out_specs,
            scratch_shapes=list(scratch),
        ),
        out_shape=out_shape,
        compiler_params=params(),
        cost_estimate=estimate,
        name=name,
    )(place, *arrays, *after)


def pack_columns(place, rows):
    tokens, width = rows.shape
    part = width // 4

    def body(at_ref, in_ref, out_ref):
        for i in range(4):
            out_ref[i] = in_ref[:, i * part : (i + 1) * part]

    return call(
        body,
        place,
        [rows],
        [pl.BlockSpec((tokens, width), lambda i, at: (0, 0))],
        pl.BlockSpec((4, tokens, part), lambda i, at: (0, 0, 0)),
        jax.ShapeDtypeStruct((4, tokens, part), rows.dtype),
        (1,),
        cost(0, 4 * tokens * width),
        "pack_columns",
    )


def pack_layers(first, second):
    tokens, layers, width = first.shape
    part = width // 4

    def body(first_ref, second_ref, out_ref):
        out_ref[0, 0] = jnp.swapaxes(first_ref[...], 0, 1)
        out_ref[0, 1] = jnp.swapaxes(second_ref[...], 0, 1)

    piece = pl.BlockSpec((tokens, layers, part), lambda i: (0, 0, i))
    return pl.pallas_call(
        body,
        grid=(4,),
        in_specs=[piece, piece],
        out_specs=pl.BlockSpec((1, 2, layers, tokens, part), lambda i: (i, 0, 0, 0, 0)),
        out_shape=jax.ShapeDtypeStruct((4, 2, layers, tokens, part), first.dtype),
        compiler_params=pltpu.CompilerParams(vmem_limit_bytes=60 * 1024 * 1024),
        cost_estimate=cost(0, 8 * tokens * layers * width),
        name="pack_layers",
    )(first, second)


def own_quarter(place, rows, after=()):
    count, width = rows.shape

    def body(at_ref, in_ref, out_ref):
        out_ref[...] = in_ref[...]

    return call(
        body,
        place,
        [rows],
        [pl.BlockSpec((count // 4, width), lambda i, at: (2 * at[1] + at[3], 0))],
        pl.BlockSpec((count // 4, width), lambda i, at: (0, 0)),
        jax.ShapeDtypeStruct((count // 4, width), rows.dtype),
        (1,),
        cost(0, count * width),
        "own_quarter",
        after=after,
    )


def stack(place, arrays, after=()):
    shape = arrays[0].shape
    zeros = (0,) * len(shape)

    def body(at_ref, *refs):
        *in_refs, out_ref = refs
        for i, ref in enumerate(in_refs):
            out_ref[i] = ref[...]

    return call(
        body,
        place,
        arrays,
        [pl.BlockSpec(shape, lambda i, at: zeros)] * len(arrays),
        pl.BlockSpec((len(arrays),) + shape, lambda i, at: (0,) + zeros),
        jax.ShapeDtypeStruct((len(arrays),) + shape, arrays[0].dtype),
        (1,),
        cost(0, 4 * len(arrays) * arrays[0].size),
        "stack",
        after=after,
    )


def key_places(i, z, shift):
    own = lax.rem(z + 4 - shift, 4)
    places = []
    for back in range(BACK):
        if back == 0:
            at = i
        elif back == 4:
            at = i - 1
        else:
            at = jnp.where(own < back, i - 1, i)
        places.append(((shift + back) % 4, jnp.maximum(at, 0)))
    return own, places


def mask_bias(i, z, start_row):
    block = 4 * i + z
    inside = lax.broadcasted_iota(jnp.int32, (BLOCK, BLOCK), 0)
    query_at = block * BLOCK + lax.broadcasted_iota(jnp.int32, (BLOCK, BLOCK), 1)
    start = jnp.broadcast_to(start_row, (BLOCK, BLOCK))
    pieces = []
    for back in range(BACK):
        key_at = (block - back) * BLOCK + inside
        allowed = key_at >= start
        if back == 0:
            allowed = allowed & (key_at <= query_at)
        pieces.append(jnp.where(allowed, 0.0, MASKED).astype(f32))
    return jnp.concatenate(pieces, axis=0)


def head_rows(ref, kv):
    return jnp.concatenate(
        [
            ref[0, 0, layer, :, pl.ds((4 * kv + head) * HD, HD)]
            for layer in range(2)
            for head in range(4)
        ],
        axis=0,
    )


def exp_scores(keys, queries, bias):
    scores = lax.dot_general(keys, queries, (((1,), (1,)), ((), ())), preferred_element_type=f32)
    copies = queries.shape[0] // BLOCK
    scores = scores * (HD**-0.5 * LOG2E) + jnp.concatenate([bias] * copies, axis=1)
    exps = jnp.exp2(scores - jnp.max(scores, axis=0, keepdims=True))
    return exps, 1.0 / jnp.sum(exps, axis=0, keepdims=True)


def value_grad_kernel(
    at_ref, start_ref, q_ref, g_ref, key_ref, out_ref, head_ref, acc
):
    i = pl.program_id(0)
    z = at_ref[0]

    @pl.when(i == 0)
    def _():
        acc[...] = jnp.zeros_like(acc)

    own, places = key_places(i, z, 0)
    bias = mask_bias(i, own, start_ref[4 * i + own])
    contribs = []
    for kv in range(2):
        keys = jnp.concatenate(
            [key_ref[held, at, :, pl.ds(kv * HD, HD)] for held, at in places], axis=0
        )
        exps, inverse = exp_scores(keys, head_rows(q_ref, kv), bias)
        probabilities = (exps * inverse).astype(bf16)
        contribs.append(
            jnp.dot(probabilities, head_rows(g_ref, kv), preferred_element_type=f32)
        )
    for kv, contrib in enumerate(contribs):
        for back, (held, at) in enumerate(places):
            acc[held, at, :, pl.ds(kv * HD, HD)] += contrib[back * BLOCK : (back + 1) * BLOCK]

    @pl.when(i == 3)
    def _():
        for held in range(4):
            out_ref[lax.rem(z + 4 - held, 4)] = acc[held].astype(bf16)
        head_ref[...] = key_ref[:, :, :, pl.ds(pl.multiple_of((z // 2) * HD, HD), HD)]


def attention_kernel(
    at_ref, start_ref, q0, q1, q2, q3, key_ref, v0, v1, v2, v3, out_ref
):
    i = pl.program_id(0)
    z = at_ref[0]
    for shift, q_ref in enumerate((q0, q1, q2, q3)):
        own, places = key_places(i, z, shift)
        bias = mask_bias(i, own, start_ref[4 * i + own])
        keys = jnp.concatenate([key_ref[held, at] for held, at in places], axis=0)
        values = jnp.concatenate([(v0, v1, v2, v3)[held][at] for held, at in places], axis=0)
        queries = jnp.concatenate(
            [
                (q_ref[0, 0] if shift == 0 else q_ref[0])[layer, :, head * HD : (head + 1) * HD]
                for layer in range(2)
                for head in range(2)
            ],
            axis=0,
        )
        exps, inverse = exp_scores(keys, queries, bias)
        mixed = lax.dot_general(
            values, exps.astype(bf16), (((0,), (0,)), ((), ())), preferred_element_type=f32
        )
        mixed = mixed * inverse
        for layer in range(2):
            for head in range(2):
                at = (2 * layer + head) * BLOCK
                out_ref[layer, 0, own, :, pl.ds(head * HD, HD)] = (
                    mixed[:, at : at + BLOCK].T.astype(bf16)
                )


SCORES = 8 * BACK * BLOCK * 8 * BLOCK
STARTS = pl.BlockSpec((16, 1, BLOCK), lambda i, at: (0, 0, 0))


def value_grad_parts(place, start, heads_and_grads, keys, after=()):
    whole = pl.BlockSpec((4, 4, BLOCK, 2 * HD), lambda i, at: (0, 0, 0, 0))
    heads = [
        pl.BlockSpec((1, 1, 2, BLOCK, 8 * HD), lambda i, at, which=which: (i, which, 0, 0, 0))
        for which in range(2)
    ]
    return call(
        value_grad_kernel,
        place,
        [start, heads_and_grads, heads_and_grads, keys],
        [STARTS] + heads + [whole],
        [whole, pl.BlockSpec((4, 4, BLOCK, HD), lambda i, at: (0, 0, 0, 0))],
        [
            jax.ShapeDtypeStruct((4, 4, BLOCK, 2 * HD), bf16),
            jax.ShapeDtypeStruct((4, 4, BLOCK, HD), bf16),
        ],
        (4,),
        cost(4 * HD * SCORES, 6 << 20, SCORES),
        "value_grad_parts",
        after=after,
        scratch=[pltpu.VMEM((4, 4, BLOCK, 2 * HD), f32)],
    )


def split_queries(place, heads_and_grads, after=()):
    def body(at_ref, in_ref, *out_refs):
        for shift, out in enumerate(out_refs, 1):
            pair = lax.rem(at_ref[0] + shift, 4)
            out[0] = in_ref[0, 0, :, :, pl.ds(pl.multiple_of(pair * 2 * HD, 2 * HD), 2 * HD)]

    piece = pl.BlockSpec((1, 2, BLOCK, 2 * HD), lambda i, at: (i, 0, 0, 0))
    return call(
        body,
        place,
        [heads_and_grads],
        [pl.BlockSpec((1, 1, 2, BLOCK, 8 * HD), lambda i, at: (i, 0, 0, 0, 0))],
        [piece] * 3,
        [jax.ShapeDtypeStruct((4, 2, BLOCK, 2 * HD), bf16)] * 3,
        (4,),
        cost(0, 4 << 20),
        "split_queries",
        after=after,
    )


def split_columns(place, rows, after=()):
    tokens, width = rows.shape
    part = width // 4

    def body(at_ref, *refs):
        for in_ref, out_ref in zip(refs[:4], refs[4:]):
            out_ref[...] = in_ref[...]

    return call(
        body,
        place,
        [rows] * 4,
        [
            pl.BlockSpec((tokens, part), lambda i, at, shift=shift: (0, lax.rem(at[2] + shift, 4)))
            for shift in range(4)
        ],
        [pl.BlockSpec((tokens, part), lambda i, at: (0, 0))] * 4,
        [jax.ShapeDtypeStruct((tokens, part), rows.dtype)] * 4,
        (1,),
        cost(0, 4 * tokens * width),
        "split_columns",
        after=after,
    )


def place_tokens(x, pieces, out_ref):
    for shift, piece in enumerate(pieces):
        at = pl.multiple_of(lax.rem(x + 4 - shift, 4) * BLOCK, BLOCK)
        out_ref[pl.ds(at, BLOCK), :] = piece[...]


def attend(place, start, queries, keys, values):
    block = pl.BlockSpec((1, 2, BLOCK, 2 * HD), lambda i, at: (i, 0, 0, 0))
    return pl.pallas_call(
        attention_kernel,
        grid_spec=pltpu.PrefetchScalarGridSpec(
            num_scalar_prefetch=1,
            grid=(4,),
            in_specs=[
                STARTS,
                pl.BlockSpec((1, 1, 2, BLOCK, 2 * HD), lambda i, at: (i, 0, 0, 0, at[0])),
            ]
            + [block] * 3
            + [pl.BlockSpec((4, 4, BLOCK, HD), lambda i, at: (0, 0, 0, 0))]
            + [pl.BlockSpec((4, BLOCK, HD), lambda i, at: (0, 0, 0))] * 4,
            out_specs=pl.BlockSpec((2, 1, 4, BLOCK, 2 * HD), lambda i, at: (0, i, 0, 0, 0)),
        ),
        out_shape=jax.ShapeDtypeStruct((2, 4, 4, BLOCK, 2 * HD), bf16),
        compiler_params=params(),
        cost_estimate=cost(4 * HD * SCORES, 6 << 20, SCORES),
        name="attend",
    )(place, start, *queries, keys, *values)


def value_parts_kernel(at_ref, h0, h1, h2, h3, w_ref, mine_ref, near_ref, far_ref, *refs):
    *out_refs, h_all, w_all = refs

    @pl.when(pl.program_id(0) == 0)
    def _():
        place_tokens(at_ref[2], (h0, h1, h2, h3), h_all)

    z = at_ref[0]
    core = at_ref[1]
    odd = at_ref[3]
    rows = w_ref.shape[0]
    quarter = rows // 4
    w_all[pl.ds(pl.multiple_of(z * rows, 16), rows), :] = w_ref[...]
    for shift in (1, 2, 3):
        base = lax.rem(z + 4 - shift, 4) * rows
        for piece, whose in (
            (mine_ref[shift - 1], 2 * core + odd),
            (near_ref[shift - 1], 2 * core + 1 - odd),
            (far_ref[0, shift - 1], 2 * (1 - core) + odd),
            (far_ref[1, shift - 1], 2 * (1 - core) + 1 - odd),
        ):
            at = pl.multiple_of(base + whose * quarter, 16)
            w_all[pl.ds(at, quarter), :] = piece
    part = jnp.dot(h_all[...], w_all[...], preferred_element_type=f32)
    part = (part * D**-0.5).astype(bf16)
    for shift, out in enumerate(out_refs):

        @pl.when(pl.program_id(0) == shift)
        def _():
            out[...] = part


def value_parts(place, features, weight_rows, mine, near, far, after=()):
    tokens = 4 * BLOCK
    rows, channels = weight_rows.shape
    piece = pl.BlockSpec((3, rows // 4, 256), lambda n, at: (0, 0, lax.rem(at[2] + n, 4)))
    return call(
        value_parts_kernel,
        place,
        [*features, weight_rows, mine, near, far],
        [pl.BlockSpec((BLOCK, FEATS), lambda n, at: (0, 0))] * 4
        + [
            pl.BlockSpec((rows, 256), lambda n, at: (0, lax.rem(at[2] + n, 4))),
            piece,
            piece,
            pl.BlockSpec((2, 3, rows // 4, 256), lambda n, at: (0, 0, 0, lax.rem(at[2] + n, 4))),
        ],
        [pl.BlockSpec((tokens, 256), lambda n, at: (0, 0))] * 4
        + [pl.BlockSpec((tokens, FEATS), lambda n, at: (0, 0))],
        [jax.ShapeDtypeStruct((tokens, 256), bf16)] * 4
        + [jax.ShapeDtypeStruct((tokens, FEATS), bf16)],
        (channels // 256,),
        cost(2 * tokens * FEATS * channels, 7 << 20),
        "value_parts",
        scratch=[pltpu.VMEM((FEATS, 256), bf16)],
        after=after,
    )


def sum_values(place, parts):
    tokens = parts[0].shape[0]

    def body(at_ref, p0, p1, p2, p3, *out_refs):
        total = (p0[...].astype(f32) + p1[...].astype(f32)) + (
            p2[...].astype(f32) + p3[...].astype(f32)
        )
        total = total.astype(bf16).reshape(4, BLOCK, 2 * HD)
        for shift, out in enumerate(out_refs):
            low = lax.rem(at_ref[0] + shift, 4) < 2
            out[...] = jnp.where(low, total[:, :, :HD], total[:, :, HD:])

    piece = pl.BlockSpec((4, BLOCK, HD), lambda i, at: (0, 0, 0))
    return pl.pallas_call(
        body,
        grid_spec=pltpu.PrefetchScalarGridSpec(
            num_scalar_prefetch=1,
            grid=(1,),
            in_specs=[pl.BlockSpec((tokens, 2 * HD), lambda i, at: (0, 0))] * 4,
            out_specs=[piece] * 4,
        ),
        out_shape=[jax.ShapeDtypeStruct((4, BLOCK, HD), bf16)] * 4,
        compiler_params=params(),
        cost_estimate=cost(1 << 19, 3 << 19),
        name="sum_values",
    )(place, *parts)


def sum_transposed(place, parts, after=()):
    def body(at_ref, in_ref, out_ref):
        for block in range(4):
            total = (in_ref[0, block].astype(f32) + in_ref[1, block].astype(f32)) + (
                in_ref[2, block].astype(f32) + in_ref[3, block].astype(f32)
            )
            out_ref[:, block * BLOCK : (block + 1) * BLOCK] = total.T.astype(bf16)

    return call(
        body,
        place,
        [parts],
        [pl.BlockSpec((4, 4, BLOCK, 2 * HD), lambda i, at: (0, 0, 0, 0))],
        pl.BlockSpec((2 * HD, 4 * BLOCK), lambda i, at: (0, 0)),
        jax.ShapeDtypeStruct((2 * HD, 4 * BLOCK), bf16),
        (1,),
        cost(1 << 19, 5 << 18),
        "sum_transposed",
        after=after,
    )


def gradient_kernel(at_ref, g0, g1, g2, g3, h_ref, keep_ref, send_ref):
    x = at_ref[2]
    low = at_ref[1] == 0
    features = h_ref[...]
    for shift, piece in enumerate((g0, g1, g2, g3)):
        owner = lax.rem(x + 4 - shift, 4)
        part = jnp.dot(piece[...], features, preferred_element_type=f32) * D**-0.5
        for pair in range(2):
            first = part[pair * 128 : pair * 128 + 64].astype(bf16)
            second = part[pair * 128 + 64 : pair * 128 + 128].astype(bf16)
            y = 2 * lax.rem(owner, 2) + pair
            keep_ref[y, owner // 2] = jnp.where(low, first, second)
            send_ref[y, owner // 2] = jnp.where(low, second, first)


def gradient_parts(place, pieces, features, after=()):
    tokens = 4 * BLOCK
    out = pl.BlockSpec((4, 2, 64, 256), lambda n, at: (0, 0, 0, n))
    return call(
        gradient_kernel,
        place,
        [*pieces, features],
        [pl.BlockSpec((2 * HD, tokens), lambda n, at: (0, 0))] * 4
        + [pl.BlockSpec((tokens, 256), lambda n, at: (0, n))],
        [out, out],
        [jax.ShapeDtypeStruct((4, 2, 64, FEATS), bf16)] * 2,
        (FEATS // 256,),
        cost(2 * tokens * FEATS * 1024, 7 << 20),
        "gradient_parts",
        after=after,
    )


def add(place, first, second, after=()):
    shape = first.shape
    block = pl.BlockSpec((1,) + shape[1:], lambda i, at: (i,) + (0,) * (len(shape) - 1))

    def body(at_ref, first_ref, second_ref, out_ref):
        total = first_ref[...].astype(f32) + second_ref[...].astype(f32)
        out_ref[...] = total.astype(bf16)

    return call(
        body,
        place,
        [first, second],
        [block, block],
        block,
        jax.ShapeDtypeStruct(shape, bf16),
        (shape[0],),
        cost(first.size, 6 * first.size),
        "add",
        after=after,
    )


def sum_and_split(place, parts, after=()):
    width = FEATS // 4

    def body(at_ref, in_ref, out_ref):
        total = (in_ref[0, 0].astype(f32) + in_ref[1, 0].astype(f32)) + (
            in_ref[2, 0].astype(f32) + in_ref[3, 0].astype(f32)
        )
        for z in range(4):
            out_ref[z] = total[:, z * width : (z + 1) * width].astype(bf16)

    return call(
        body,
        place,
        [parts],
        [pl.BlockSpec((4, 1, 64, FEATS), lambda i, at: (0, i, 0, 0))],
        pl.BlockSpec((4, 64, width), lambda i, at: (i, 0, 0)),
        jax.ShapeDtypeStruct((8, 64, width), bf16),
        (2,),
        cost(1 << 20, 5 << 19),
        "sum_and_split",
        after=after,
    )


def update(place, parts, master, first_moment, second_moment, after=()):
    rows, width = master.shape

    def body(at_ref, parts_ref, master_ref, first_ref, second_ref, m_out, a_out, b_out, w_out):
        gradient = parts_ref[0].astype(f32)
        for i in range(1, 8):
            gradient = gradient + parts_ref[i].astype(f32)
        new_master, new_first, new_second = adam_update(
            gradient, master_ref[...], first_ref[...], second_ref[...]
        )
        m_out[...] = new_master
        a_out[...] = new_first
        b_out[...] = new_second
        for i in range(8):
            w_out[i] = new_master.astype(bf16)

    state = pl.BlockSpec((rows, width), lambda i, at: (0, 0))
    eight = pl.BlockSpec((8, rows, width), lambda i, at: (0, 0, 0))
    return call(
        body,
        place,
        [parts, master, first_moment, second_moment],
        [eight, state, state, state],
        [state, state, state, eight],
        [jax.ShapeDtypeStruct((rows, width), f32)] * 3
        + [jax.ShapeDtypeStruct((8, rows, width), bf16)],
        (1,),
        cost(1 << 20, 2 << 20),
        "update",
        after=after,
    )


def join_cores(place, mine, other, after=()):
    count, rows, width = mine.shape

    def body(at_ref, mine_ref, other_ref, out_ref):
        low = at_ref[1] == 0
        for at in range(count):
            a = mine_ref[at].astype(f32)
            b = other_ref[at].astype(f32)
            both = jnp.concatenate([jnp.where(low, a, b), jnp.where(low, b, a)], axis=0)
            out_ref[:, pl.ds(at * 2 * rows, 2 * rows)] = both.T.astype(bf16)

    return call(
        body,
        place,
        [mine, other],
        [pl.BlockSpec(mine.shape, lambda i, at: (0, 0, 0))] * 2,
        pl.BlockSpec((width, 2 * count * rows), lambda i, at: (0, 0)),
        jax.ShapeDtypeStruct((width, 2 * count * rows), bf16),
        (1,),
        cost(0, 2 << 20),
        "join_cores",
        after=after,
    )


def exchange(parts, axes):
    return lax.all_to_all(parts, axes, split_axis=0, concat_axis=0, tiled=True)


def from_lower(array, axis, shift):
    return lax.ppermute(array, axis, [(i, (i + shift) % 4) for i in range(4)])


def swap_cores(array):
    return lax.ppermute(array, "core", [(0, 1), (1, 0)])


def per_device(
    hidden, queries, keys, cotangent, segments, weight, master, first_moment, second_moment
):
    x, y, z, core = (lax.axis_index(name) for name in ("x", "y", "z", "core"))
    odd = lax.rem(y, 2)
    place = jnp.stack([z, core, x, odd]).astype(jnp.int32)

    documents = jnp.arange(8, dtype=jnp.int32)
    first_of = jnp.sum((segments[0][None, :] < documents[:, None]).astype(jnp.int32), axis=1)
    start = jnp.sum(
        jnp.where(segments[0][None, :] == documents[:, None], first_of[:, None], 0), axis=0
    ).reshape(16, 1, BLOCK)

    own_keys = exchange(pack_columns(place, keys[0]), "x")
    packed = pack_layers(queries[0], cotangent[0])
    heads_and_grads = exchange(packed, "x")
    all_keys = stack(
        place, [own_keys] + [from_lower(own_keys, "z", shift) for shift in (1, 2, 3)]
    )

    weight_rows = weight.T
    sent_quarter = own_quarter(place, weight_rows, after=[own_keys])
    mine = stack(place, [from_lower(sent_quarter, "z", shift) for shift in (1, 2, 3)])

    grad_parts, key_heads = value_grad_parts(
        place, start, heads_and_grads, all_keys, after=[mine]
    )
    grad_moved = exchange(grad_parts, "z")

    features_to = split_columns(place, hidden[0], after=[grad_parts])
    own_features = [features_to[0]] + [
        from_lower(features_to[shift], "x", shift) for shift in (1, 2, 3)
    ]
    queries_to = split_queries(place, heads_and_grads, after=[grad_parts])
    queries_from = [heads_and_grads] + [
        from_lower(piece, "z", shift) for shift, piece in enumerate(queries_to, 1)
    ]

    grad_rows = sum_transposed(place, grad_moved)
    pieces = [grad_rows] + [from_lower(grad_rows, "x", shift) for shift in (1, 2, 3)]

    near = lax.ppermute(mine, "y", [(0, 1), (1, 0), (2, 3), (3, 2)])
    far = swap_cores(stack(place, [mine, near], after=[grad_parts]))
    *parts_to, all_features = value_parts(place, own_features, weight_rows, mine, near, far)
    parts_from = [parts_to[0]] + [from_lower(parts_to[shift], "x", shift) for shift in (1, 2, 3)]
    values = sum_values(place, parts_from)
    values_from = [values[0]] + [from_lower(values[shift], "z", shift) for shift in (1, 2, 3)]

    keep, send = gradient_parts(
        place, pieces, all_features, after=[queries_from[1], queries_from[3]]
    )
    both = add(place, keep, swap_cores(send))
    split = sum_and_split(
        place, exchange(both, "y"), after=[queries_from[2]] + values_from[1:]
    )
    by_feature = exchange(split, ("zh", "z"))
    attention = attend(place, start, queries_from, key_heads, values_from)
    new_master, new_first, new_second, shard = update(
        place, by_feature, master, first_moment, second_moment, after=[attention]
    )
    shards = exchange(shard, ("zh", "y"))
    fresh = join_cores(place, shards, swap_cores(shards)).T
    attention = attention.reshape(1, 2, 16 * BLOCK, 2 * HD)
    return (attention, new_master, new_first, new_second, fresh)


def solution(mesh):
    fine = Mesh(mesh.devices.reshape(2, 4, 2, 4, 4), DP + SEQ)
    in_specs = (
        P(DP, SEQ, None),
        P(DP, SEQ, None, None),
        P(DP, SEQ, None),
        P(DP, SEQ, None, None),
        P(DP, None),
        P(None, SEQ),
        P(DP, SEQ),
        P(DP, SEQ),
        P(DP, SEQ),
    )
    out_specs = (
        P(DP, None, None, SEQ),
        P(DP, SEQ),
        P(DP, SEQ),
        P(DP, SEQ),
        P(None, SEQ),
    )
    return jax.shard_map(
        per_device, mesh=fine, in_specs=in_specs, out_specs=out_specs, check_vma=False
    )
```
